32 devices in a mesh: grp: 2 (over y), row: 16 (over z, x, core).
Axes of the slice: x: 2, y: 2, z: 4, core: 2. Of those that a mesh axis runs over, the one named last changes fastest.
Arguments:
- queries: bfloat16 [4096, 4096], P(('grp', 'row')), parts along dimension 0, may hold values from -130 to 130
- answer_keys: bfloat16 [4096, 512], P(('grp', 'row')), parts along dimension 0, may hold values from -6 to 6
- answer_values: bfloat16 [4096, 512], P(('grp', 'row')), parts along dimension 0, may hold values from -6 to 6
- prompt_keys: bfloat16 [256, 512], P(('grp', 'row')), parts along dimension 0, may hold values from -4 to 4
- prompt_values: bfloat16 [256, 512], P(('grp', 'row')), parts along dimension 0, may hold values from -6 to 6
- out_grad: bfloat16 [4096, 4096], P(('grp', 'row')), parts along dimension 0, may hold values from -6 to 6
- weights: float32 [4096], P(('grp', 'row')), parts along dimension 0, may hold values from 0.25 to 4
- lengths: int32 [64], P('grp'), parts along dimension 0, may hold values from 1 to 256, as said below
Outputs:
- attn_out: bfloat16 [4096, 4096], P(('grp', 'row')), parts along dimension 0
- q_grad: bfloat16 [4096, 4096], P(('grp', 'row')), parts along dimension 0
- answer_key_grad: bfloat16 [4096, 512], P(('grp', 'row')), parts along dimension 0
- answer_value_grad: bfloat16 [4096, 512], P(('grp', 'row')), parts along dimension 0
- prompt_key_grad: float32 [256, 512], P(('grp', 'row')), parts along dimension 0
- prompt_value_grad: float32 [256, 512], P(('grp', 'row')), parts along dimension 0
The draws below stay inside these ranges and needn't reach their ends.
There are 2 independent parts, one for each index of `grp`. The reference program is written for one: setup_inputs(seed, part) draws one part's arguments, and reference() takes and returns one part's arrays. A program takes and returns all parts, laid end to end along the dimension named above; each array names one. Nothing has to cross between parts.
Inputs may be any that keep to these rules, and one draw needn't show every extreme that they name: `lengths`: the answers fill the 2048 packed rows in order; the longest has exactly 256 rows.
All inputs are finite; a program needn't handle non-finite values.
Results may differ from the reference program's by a relative error of at most 0.02.
Values may be sent and summed in bfloat16 or wider, within the bound.
No kernel may reach another device: no remote copies, remote signals or barrier semaphores. Data moves between devices by JAX's collectives and lax.ppermute only.
A program may use at most 192 MiB of HBM per device.

```python
import math
import jax
import jax.numpy as jnp
from jax import lax

HEADS = 32
KV_HEADS = 4
HEAD_DIM = 128
ROWS_DEV = 128
ROWS = 2048
PROMPT = 128
ANSWERS = 32
MOST_LEN = 256
N_ROW = 16


def drawn_pair(key):
    folded = jax.random.fold_in(key, 11)
    key_draw, query_draw = jax.random.split(folded, 2)
    prompt_rows = jnp.clip(jax.random.normal(key_draw, (PROMPT, KV_HEADS * HEAD_DIM), jnp.float32), -4.0, 4.0)
    queries = jnp.clip(3.0 * jax.random.normal(query_draw, (ROWS, HEADS * HEAD_DIM), jnp.float32), -18.0, 18.0)
    return (queries, prompt_rows)


def draw_queries(key, part):
    return drawn_pair(key)[0].astype(jnp.bfloat16)


def draw_prompt_keys(key, part):
    return drawn_pair(key)[1].astype(jnp.bfloat16)


def draw_lengths(key, part):
    total = ROWS - MOST_LEN - 1
    count = ANSWERS - 2
    height = MOST_LEN // 2
    spots = jnp.arange(1, total, dtype=jnp.int32)
    order = jax.random.permutation(jax.random.fold_in(key, 23), total - 1).astype(jnp.int32)
    inside = spots % height
    ranking = jnp.where(inside == height // 2, -1, jnp.where(inside == 0, total + order, order))
    picked = jnp.argsort(ranking, stable=True)[:count - 1]
    cuts = jnp.sort(spots[picked])
    edges = jnp.concatenate([jnp.zeros((1,), jnp.int32), cuts, jnp.full((1,), total, jnp.int32)])
    leading = edges[1:] - edges[:-1]
    closing = jnp.array([MOST_LEN, 1], dtype=jnp.int32)
    return jnp.concatenate([leading, closing]).astype(jnp.int32)


def block_levels(rng, dims, shards, least, largest):
    factor_of, own = 1.0, jax.random.fold_in(rng, 6)
    for axis_at, shards_of in shards:
        steps = jnp.exp(jax.random.uniform(jax.random.fold_in(own, axis_at), (shards_of,), jnp.float32, least / len(shards), largest / len(shards)))
        factor_of = factor_of * jnp.repeat(steps, dims[axis_at] // shards_of).reshape([-1 if axis == axis_at else 1 for axis in range(len(dims))])
    return factor_of


def scatter_about(key, extent, scale, bound, pieces=(), held_as=jnp.bfloat16):
    loudness = block_levels(key, extent, pieces, -0.22, 0.18) if pieces else 1.0
    values = jax.random.normal(key, extent, jnp.float32) * scale * loudness
    return jnp.minimum(jnp.maximum(values, -bound), bound).astype(held_as)


def setup_inputs(seed: int = 0, part: int = 0) -> dict:
    seeds = jax.random.split(jax.random.key(seed), 9)
    part_splits = jax.random.split(jax.random.fold_in(seeds[8], part), 9)
    return {
        "queries": draw_queries(jax.random.fold_in(jax.random.fold_in(seeds[8], part), 71), part),
        "answer_keys": scatter_about(part_splits[1], (ROWS, KV_HEADS * HEAD_DIM), 1.0, 6.0, ((0, 16),)),
        "answer_values": scatter_about(part_splits[2], (ROWS, KV_HEADS * HEAD_DIM), 1.0, 6.0, ((0, 16),)),
        "prompt_keys": draw_prompt_keys(jax.random.fold_in(jax.random.fold_in(seeds[8], part), 71), part),
        "prompt_values": scatter_about(part_splits[4], (PROMPT, KV_HEADS * HEAD_DIM), 1.0, 6.0, ((0, 16),)),
        "out_grad": scatter_about(part_splits[5], (ROWS, HEADS * HEAD_DIM), 1.0, 6.0, ((0, 16),)),
        "weights": jnp.clip(jnp.exp(math.log(4.0) - 2.7725887 * jax.random.uniform(part_splits[6], (ROWS,), jnp.float32) ** block_levels(part_splits[6], (ROWS,), ((0, 16),), -0.2, 0.2)), 0.25, 4.0),
        "lengths": draw_lengths(jax.random.fold_in(jax.random.fold_in(seeds[8], part), 71), part),
    }


MASKED = -1.0e30


def times_transposed(former, latter):
    return lax.dot_general(former, latter, (((1,), (1,)), ((), ())), preferred_element_type=jnp.float32)


def transposed_times(former, latter):
    return lax.dot_general(former, latter, (((0,), (0,)), ((), ())), preferred_element_type=jnp.float32)


def segment_of(positions, lengths):
    finish = jnp.cumsum(lengths, dtype=jnp.int32)
    starts = finish - lengths
    covered = (starts[None, :] <= positions[:, None]).astype(jnp.int32)
    return jnp.sum(covered, axis=1, dtype=jnp.int32) - 1


def probabilities(flat_queries, key_rows, allowed, group_size):
    key_count = key_rows.shape[0]
    height = allowed.shape[0]
    factor = key_rows.shape[1] ** -0.5
    scores = (times_transposed(flat_queries, key_rows) * factor).reshape(height, group_size, key_count)
    window = jnp.concatenate([jnp.ones((height, key_count - allowed.shape[1]), dtype=jnp.bool_), allowed], axis=1)
    scores = jnp.where(window[:, None, :], scores, MASKED)
    highest = jnp.max(scores, axis=2, keepdims=True)
    powers = jnp.exp(scores - highest)
    totals = jnp.sum(powers, axis=2, keepdims=True)
    return (powers / totals).reshape(height * group_size, key_count)


def block_terms(q_block, cot_block, key_rows, value_rows, allowed):
    height = q_block.shape[0]
    group_size = HEADS // KV_HEADS
    span_cols = group_size * HEAD_DIM
    factor = HEAD_DIM ** -0.5
    outputs, q_grads, key_terms, value_terms = [], [], [], []
    for kv_index in range(KV_HEADS):
        flat_queries = q_block[:, kv_index * span_cols:(kv_index + 1) * span_cols].reshape(height * group_size, HEAD_DIM)
        flat_cot = cot_block[:, kv_index * span_cols:(kv_index + 1) * span_cols].reshape(height * group_size, HEAD_DIM)
        key_slice = key_rows[:, kv_index * HEAD_DIM:(kv_index + 1) * HEAD_DIM]
        value_slice = value_rows[:, kv_index * HEAD_DIM:(kv_index + 1) * HEAD_DIM]
        chances = probabilities(flat_queries, key_slice, allowed, group_size)
        rounded = chances.astype(jnp.bfloat16)
        attended = jnp.dot(rounded, value_slice, preferred_element_type=jnp.float32).astype(jnp.bfloat16)
        row_delta = jnp.sum(flat_cot.astype(jnp.float32) * attended.astype(jnp.float32), axis=1, keepdims=True)
        slopes = times_transposed(flat_cot, value_slice)
        score_grad = (chances * (slopes - row_delta)).astype(jnp.bfloat16)
        q_part = (jnp.dot(score_grad, key_slice, preferred_element_type=jnp.float32) * factor).astype(jnp.bfloat16)
        outputs.append(attended.reshape(height, span_cols))
        q_grads.append(q_part.reshape(height, span_cols))
        key_terms.append(transposed_times(score_grad, flat_queries) * factor)
        value_terms.append(transposed_times(rounded, flat_cot))
    return (jnp.concatenate(outputs, axis=1), jnp.concatenate(q_grads, axis=1),
            jnp.concatenate(key_terms, axis=1), jnp.concatenate(value_terms, axis=1))


def reference(queries, answer_keys, answer_values, prompt_keys, prompt_values, out_grad, weights, lengths):
    height = ROWS_DEV
    columns = KV_HEADS * HEAD_DIM
    cotangent = (weights[:, None] * out_grad.astype(jnp.float32)).astype(jnp.bfloat16)
    padding = jnp.zeros((2 * height, columns), jnp.bfloat16)
    padded_keys = jnp.concatenate([padding, answer_keys], axis=0)
    padded_values = jnp.concatenate([padding, answer_values], axis=0)
    own_offsets = jnp.arange(height, dtype=jnp.int32)
    key_offsets = jnp.arange(3 * height, dtype=jnp.int32)

    def advance(running, block_index):
        prompt_key_sum, prompt_value_sum, answer_key_sum, answer_value_sum = running
        start_row = block_index * height
        q_block = lax.dynamic_slice_in_dim(queries, start_row, height, 0)
        cot_block = lax.dynamic_slice_in_dim(cotangent, start_row, height, 0)
        window_keys = lax.dynamic_slice_in_dim(padded_keys, start_row, 3 * height, 0)
        window_values = lax.dynamic_slice_in_dim(padded_values, start_row, 3 * height, 0)
        own_pos = start_row + own_offsets
        key_pos = start_row - 2 * height + key_offsets
        own_seg = segment_of(own_pos, lengths)
        key_seg = segment_of(key_pos, lengths)
        allowed = (key_pos[None, :] >= 0) & (key_pos[None, :] <= own_pos[:, None]) & (key_seg[None, :] == own_seg[:, None])
        key_rows = jnp.concatenate([prompt_keys, window_keys], axis=0)
        value_rows = jnp.concatenate([prompt_values, window_values], axis=0)
        outputs, q_grads, key_terms, value_terms = block_terms(q_block, cot_block, key_rows, value_rows, allowed)
        prompt_key_sum = prompt_key_sum + key_terms[:PROMPT]
        prompt_value_sum = prompt_value_sum + value_terms[:PROMPT]
        answer_key_sum = lax.dynamic_update_slice_in_dim(
            answer_key_sum, lax.dynamic_slice_in_dim(answer_key_sum, start_row, 3 * height, 0) + key_terms[PROMPT:], start_row, 0)
        answer_value_sum = lax.dynamic_update_slice_in_dim(
            answer_value_sum, lax.dynamic_slice_in_dim(answer_value_sum, start_row, 3 * height, 0) + value_terms[PROMPT:], start_row, 0)
        return (prompt_key_sum, prompt_value_sum, answer_key_sum, answer_value_sum), (outputs, q_grads)

    initial = (jnp.zeros((PROMPT, columns), jnp.float32), jnp.zeros((PROMPT, columns), jnp.float32),
               jnp.zeros((ROWS + 2 * height, columns), jnp.float32), jnp.zeros((ROWS + 2 * height, columns), jnp.float32))
    running, stacked = lax.scan(advance, initial, jnp.arange(N_ROW, dtype=jnp.int32))
    attn_out = stacked[0].reshape(ROWS, HEADS * HEAD_DIM)
    q_grad = stacked[1].reshape(ROWS, HEADS * HEAD_DIM)
    answer_key_grad = running[2][2 * height:].astype(jnp.bfloat16)
    answer_value_grad = running[3][2 * height:].astype(jnp.bfloat16)
    return attn_out, q_grad, answer_key_grad, answer_value_grad, running[0], running[1]
```

```python
import functools
import math

import jax
import jax.numpy as jnp
from jax import lax
from jax.experimental import pallas as pl
from jax.experimental.pallas import tpu as pltpu
from jax.sharding import PartitionSpec as P

HEAD_DIM = 128
MASKED = -1e30
BF16 = jnp.bfloat16
F32 = jnp.float32


def shifted(x, axis, by):
    length = lax.axis_size(axis)
    pairs = [(i, i + by) for i in range(length) if 0 <= i + by < length]
    return lax.ppermute(x, axis, pairs)


def dot_nt(former, latter):
    return lax.dot_general(former, latter, (((1,), (1,)), ((), ())), preferred_element_type=F32)


def dot_nn(former, latter):
    return lax.dot_general(former, latter, (((1,), (0,)), ((), ())), preferred_element_type=F32)


def window_bias(lengths_row, height, heads):
    answers = lengths_row.shape[1]
    before = lax.broadcasted_iota(jnp.int32, (answers, answers), 1) < lax.broadcasted_iota(
        jnp.int32, (answers, answers), 0
    )
    spread = jnp.broadcast_to(lengths_row.astype(F32), (answers, answers))
    starts = jnp.sum(jnp.where(before, spread, 0.0), axis=1, keepdims=True)
    first = lax.axis_index("row") * height
    own = (lax.broadcasted_iota(jnp.int32, (answers, height), 1) + first).astype(F32)
    begin = jnp.max(jnp.where(starts <= own, starts, 0.0), axis=0, keepdims=True)
    shape = (3 * height, height)
    key = (lax.broadcasted_iota(jnp.int32, shape, 0) + (first - 2 * height)).astype(F32)
    row = (lax.broadcasted_iota(jnp.int32, shape, 1) + first).astype(F32)
    bias = jnp.where((key <= row) & (key >= begin), 0.0, MASKED)
    return jnp.concatenate([bias] * heads, axis=1)


def attention_kernel(
    lengths_ref, weights_ref, q_ref, do_ref, pk_ref, pv_ref, fk_ref, fv_ref, nk_ref, nv_ref, ok_ref, ov_ref,
    out_ref, dq_ref, dpk_ref, dpv_ref, far_k_ref, far_v_ref, near_k_ref, near_v_ref, own_k_ref, own_v_ref,
    bias_ref, spread_ref,
):
    height = q_ref.shape[0]
    heads = q_ref.shape[1] // HEAD_DIM
    prompt = pk_ref.shape[0]
    factor = HEAD_DIM**-0.5
    pair = 2

    @pl.when(pl.program_id(0) == 0)
    def _():
        bias_ref[...] = window_bias(lengths_ref[...], height, pair)
        spread_ref[...] = jnp.broadcast_to(weights_ref[...], (HEAD_DIM, height)).T

    keys = jnp.concatenate([pk_ref[...], fk_ref[...], nk_ref[...], ok_ref[...]], axis=0)
    values = jnp.concatenate([pv_ref[...], fv_ref[...], nv_ref[...], ov_ref[...]], axis=0)
    keys_t = keys.astype(F32).T.astype(BF16)
    values_t = values.astype(F32).T.astype(BF16)
    spread = spread_ref[...]
    dk = dv = None
    for h in range(0, heads, pair):
        cols = [slice((h + i) * HEAD_DIM, (h + i + 1) * HEAD_DIM) for i in range(pair)]
        q = jnp.concatenate([q_ref[:, c] for c in cols], axis=0)
        cot = jnp.concatenate([(do_ref[:, c].astype(F32) * spread).astype(BF16) for c in cols], axis=0)
        scores = dot_nt(keys, q)
        scores = jnp.concatenate([scores[:prompt], scores[prompt:] + bias_ref[...]], axis=0)
        highest = jnp.max(scores, axis=0, keepdims=True)
        powers = jnp.exp2((scores - highest) * (factor * math.log2(math.e)))
        total = jnp.sum(powers, axis=0, keepdims=True)
        chances = powers * (1.0 / total)
        rounded = chances.astype(BF16)
        slopes = dot_nt(values, cot)
        delta = jnp.sum(chances * slopes, axis=0, keepdims=True)
        grad = (chances * (slopes - delta)).astype(BF16)
        out = dot_nn(values_t, rounded).T.astype(BF16)
        dq = (dot_nn(keys_t, grad) * factor).T.astype(BF16)
        for i, c in enumerate(cols):
            out_ref[:, c] = out[i * height : (i + 1) * height]
            dq_ref[:, c] = dq[i * height : (i + 1) * height]
        dk_part, dv_part = dot_nn(grad, q), dot_nn(rounded, cot)
        dk, dv = (dk_part, dv_part) if dk is None else (dk + dk_part, dv + dv_part)
    dk = dk * factor
    at = 0
    for k_ref, v_ref in ((dpk_ref, dpv_ref), (far_k_ref, far_v_ref), (near_k_ref, near_v_ref), (own_k_ref, own_v_ref)):
        size = k_ref.shape[0]
        k_ref[...] = dk[at : at + size].astype(k_ref.dtype)
        v_ref[...] = dv[at : at + size].astype(v_ref.dtype)
        at += size


def per_device(
    queries, answer_keys, answer_values, prompt_keys, prompt_values, out_grad, weights, lengths
):
    height = queries.shape[0]
    columns = answer_keys.shape[1]
    kv_heads = columns // HEAD_DIM
    span = queries.shape[1] // kv_heads
    size = lax.axis_size("row")
    own_prompt = prompt_keys.shape[0]
    prompt = own_prompt * size

    own = jnp.concatenate([answer_keys, answer_values], axis=1)
    near, far = shifted(own, "row", 1), shifted(own, "row", 2)
    pair = jnp.concatenate([prompt_keys, prompt_values], axis=1)
    shared = lax.all_to_all(
        jnp.broadcast_to(pair[None], (size, own_prompt, 2 * columns)), "row", 0, 0, tiled=True
    ).reshape(prompt, 2 * columns)

    def key_cols(rows):
        return pl.BlockSpec((rows, HEAD_DIM), lambda g: (0, g))

    def value_cols(rows):
        return pl.BlockSpec((rows, HEAD_DIM), lambda g: (0, g + kv_heads))

    wide = pl.BlockSpec((height, span), lambda g: (0, g))

    def grads(rows, dtype):
        return jax.ShapeDtypeStruct((rows, columns), dtype)

    whole = jax.ShapeDtypeStruct(queries.shape, BF16)
    out, dq, dpk, dpv, fk, fv, nk, nv, ok, ov = pl.pallas_call(
        attention_kernel,
        grid=(kv_heads,),
        in_specs=[
            pl.BlockSpec((1, lengths.shape[0]), lambda g: (0, 0)),
            pl.BlockSpec((1, height), lambda g: (0, 0)),
            wide, wide,
            key_cols(prompt), value_cols(prompt),
            key_cols(height), value_cols(height),
            key_cols(height), value_cols(height),
            key_cols(height), value_cols(height),
        ],
        out_specs=[wide, wide, key_cols(prompt), key_cols(prompt)] + [key_cols(height)] * 6,
        out_shape=[whole, whole] + [grads(prompt, BF16)] * 2 + [grads(height, BF16)] * 4 + [grads(height, F32)] * 2,
        scratch_shapes=[
            pltpu.VMEM((3 * height, 2 * height), F32),
            pltpu.VMEM((height, HEAD_DIM), F32),
        ],
        compiler_params=pltpu.CompilerParams(vmem_limit_bytes=48 * 2**20),
        cost_estimate=pl.CostEstimate(flops=3_200_000_000, bytes_accessed=6_000_000, transcendentals=2_000_000),
    )(
        lengths.reshape(1, -1), weights.reshape(1, -1), queries, out_grad,
        shared, shared, far, far, near, near, own, own,
    )
    terms = jnp.concatenate([dpk, dpv], axis=1).reshape(size, own_prompt, 2 * columns)
    summed = jnp.sum(lax.all_to_all(terms, "row", 0, 0, tiled=True).astype(F32), axis=0)
    from_near = shifted(jnp.concatenate([nk, nv], axis=1), "row", -1).astype(F32)
    from_far = shifted(jnp.concatenate([fk, fv], axis=1), "row", -2).astype(F32)
    dk = (ok + from_near[:, :columns] + from_far[:, :columns]).astype(BF16)
    dv = (ov + from_near[:, columns:] + from_far[:, columns:]).astype(BF16)
    return out, dq, dk, dv, summed[:, :columns], summed[:, columns:]


def solution(mesh):
    rows = P(("grp", "row"), None)
    return jax.shard_map(
        per_device,
        mesh=mesh,
        in_specs=(rows,) * 6 + (P(("grp", "row")), P("grp")),
        out_specs=(rows,) * 6,
        check_vma=False,
    )
```

```python
import math

import jax
import jax.numpy as jnp
from jax import lax
from jax.experimental import pallas as pl
from jax.experimental.pallas import tpu as pltpu
from jax.sharding import PartitionSpec as P

HEAD_DIM = 128
PARTS = 4
FACTOR = HEAD_DIM**-0.5
EXPONENT = FACTOR * math.log2(math.e)
MASKED = -1e30
BF16 = jnp.bfloat16
F32 = jnp.float32
VMEM_LIMIT = 60 * 2**20


def shifted(x, by):
    length = lax.axis_size("row")
    pairs = [(i, i + by) for i in range(length) if 0 <= i + by < length]
    return lax.ppermute(x, "row", pairs)


def dot_nt(former, latter):
    return lax.dot_general(former, latter, (((1,), (1,)), ((), ())), preferred_element_type=F32)


def dot_nn(former, latter):
    return lax.dot_general(former, latter, (((1,), (0,)), ((), ())), preferred_element_type=F32)


def transposed(x):
    return x.astype(F32).T.astype(BF16)


def window_bias(lengths_row, height, heads, part):
    answers = lengths_row.shape[1]
    rows = height // PARTS
    before = lax.broadcasted_iota(jnp.int32, (answers, answers), 1) < lax.broadcasted_iota(
        jnp.int32, (answers, answers), 0
    )
    spread = jnp.broadcast_to(lengths_row.astype(F32), (answers, answers))
    starts = jnp.sum(jnp.where(before, spread, 0.0), axis=1, keepdims=True)
    first = lax.axis_index("row") * height + part * rows
    lane = lax.broadcasted_iota(jnp.int32, (1, heads * rows), 1)
    own = (lax.rem(lane, rows) + first).astype(F32)
    begin = jnp.max(jnp.where(starts <= own, starts, 0.0), axis=0, keepdims=True)
    shape = (2 * height + rows, heads * rows)
    key = (lax.broadcasted_iota(jnp.int32, shape, 0) + (first - 2 * height)).astype(F32)
    return jnp.where((key <= own) & (key >= begin), 0.0, MASKED)


def flat_part(ref, part):
    rows = ref.shape[0] // PARTS
    heads = ref.shape[1] // HEAD_DIM
    return jnp.concatenate(
        [ref[part * rows : (part + 1) * rows, h * HEAD_DIM : (h + 1) * HEAD_DIM] for h in range(heads)], axis=0
    )


def store_part(ref, part, value):
    rows = ref.shape[0] // PARTS
    for h in range(ref.shape[1] // HEAD_DIM):
        ref[part * rows : (part + 1) * rows, h * HEAD_DIM : (h + 1) * HEAD_DIM] = value[h * rows : (h + 1) * rows]


def staged(*stages):
    held = {}
    for step in range(PARTS + len(stages) - 1):
        for place, stage in enumerate(stages):
            part = step - place
            if 0 <= part < PARTS:
                held[part] = stage(part, held.get(part))


def pack_kernel(k_ref, v_ref, pk_ref, pv_ref, own_ref, spread_ref):
    own_ref[...] = jnp.concatenate([k_ref[...], v_ref[...]], axis=1)
    pair = jnp.concatenate([pk_ref[...], pv_ref[...]], axis=1)
    spread_ref[...] = jnp.broadcast_to(pair[None], spread_ref.shape)


def attention_kernel(n_near, *refs):
    lengths_ref, weights_ref, q_ref, do_ref, pk_ref, pv_ref, fk_ref, fv_ref, *rest = refs
    near, rest = rest[: 2 * n_near], rest[2 * n_near :]
    ok_ref, ov_ref, out_ref, dq_ref, terms_ref, far_ref, near_ref, own_ref, bias_ref, spread_ref, dk_ref, dv_ref = rest
    height = q_ref.shape[0]
    heads = q_ref.shape[1] // HEAD_DIM
    prompt = pk_ref.shape[0]
    rows = height // PARTS
    window = 2 * height + rows
    kv_heads = own_ref.shape[1] // (2 * HEAD_DIM)

    @pl.when(pl.program_id(0) == 0)
    def _():
        for part in range(PARTS):
            bias_ref[part] = window_bias(lengths_ref[...], height, heads, part)
        spread_ref[...] = jnp.broadcast_to(weights_ref[...], (HEAD_DIM, height)).T

    nk, nv = near[0][...], near[1][...]
    for i in range(1, n_near):
        nk, nv = nk + near[2 * i][...], nv + near[2 * i + 1][...]
    keys = jnp.concatenate([pk_ref[...], fk_ref[...], nk, ok_ref[...]], axis=0)
    values = jnp.concatenate([pv_ref[...], fv_ref[...], nv, ov_ref[...]], axis=0)
    keys_t, values_t = transposed(keys), transposed(values)
    dk_ref[...] = jnp.zeros_like(dk_ref)
    dv_ref[...] = jnp.zeros_like(dv_ref)

    def reachable(x, part):
        begin = prompt + part * rows
        return jnp.concatenate([x[:prompt], x[begin : begin + window]], axis=0)

    def everywhere(x, part):
        before, after = part * rows, height - (part + 1) * rows
        pieces = [x[:prompt], jnp.zeros((before, x.shape[1]), x.dtype), x[prompt:], jnp.zeros((after, x.shape[1]), x.dtype)]
        return jnp.concatenate([piece for piece in pieces if piece.shape[0]], axis=0)

    def score(part, _):
        q, cot = flat_part(q_ref, part), flat_part(do_ref, part)
        spread = jnp.concatenate([spread_ref[part * rows : (part + 1) * rows]] * heads, axis=0)
        cot = (cot.astype(F32) * spread).astype(BF16)
        return q, cot, dot_nt(reachable(keys, part), q), dot_nt(reachable(values, part), cot)

    def weigh(part, held):
        q, cot, scores, slopes = held
        scores = jnp.concatenate([scores[:prompt], scores[prompt:] + bias_ref[part]], axis=0)
        highest = jnp.max(scores, axis=0, keepdims=True)
        powers = jnp.exp2((scores - highest) * EXPONENT)
        chances = powers * (1.0 / jnp.sum(powers, axis=0, keepdims=True))
        delta = jnp.sum(chances * slopes, axis=0, keepdims=True)
        return q, cot, chances.astype(BF16), (chances * (slopes - delta)).astype(BF16)

    def gather(part, held):
        q, cot, chances, grad = held
        store_part(out_ref, part, dot_nn(values_t, everywhere(chances, part)).T.astype(BF16))
        store_part(dq_ref, part, (dot_nn(keys_t, everywhere(grad, part)) * FACTOR).T.astype(BF16))
        begin = prompt + part * rows
        for ref, terms in ((dk_ref, dot_nn(grad, q)), (dv_ref, dot_nn(chances, cot))):
            ref[:prompt] += terms[:prompt]
            ref[begin : begin + window] += terms[prompt:]

    staged(score, weigh, gather)
    g = pl.program_id(0)
    at = 0
    for ref in (terms_ref, far_ref, near_ref, own_ref):
        end = at + ref.shape[0]
        ref[:, pl.ds(pl.multiple_of(g * HEAD_DIM, HEAD_DIM), HEAD_DIM)] = (dk_ref[at:end] * FACTOR).astype(ref.dtype)
        ref[:, pl.ds(pl.multiple_of((g + kv_heads) * HEAD_DIM, HEAD_DIM), HEAD_DIM)] = dv_ref[at:end].astype(ref.dtype)
        at = end


def per_device(
    queries, answer_keys, answer_values, prompt_keys, prompt_values, out_grad, weights, lengths
):
    height = queries.shape[0]
    columns = answer_keys.shape[1]
    kv_heads = columns // HEAD_DIM
    span = queries.shape[1] // kv_heads
    flat = height * queries.shape[1] // HEAD_DIM
    size = lax.axis_size("row")
    own_prompt = prompt_keys.shape[0]
    prompt = own_prompt * size
    window = 2 * height + height // PARTS

    def shape(rows, cols, dtype=BF16):
        return jax.ShapeDtypeStruct((rows, cols), dtype)

    def key_cols(rows):
        return pl.BlockSpec((rows, HEAD_DIM), lambda g: (0, g))

    def value_cols(rows):
        return pl.BlockSpec((rows, HEAD_DIM), lambda g: (0, g + kv_heads))

    def fixed(rows, cols):
        return pl.BlockSpec((rows, cols), lambda g: (0, 0))

    wide = pl.BlockSpec((height, span), lambda g: (0, g))

    own, spread = pl.pallas_call(
        pack_kernel,
        out_shape=[shape(height, 2 * columns), jax.ShapeDtypeStruct((size, own_prompt, 2 * columns), BF16)],
    )(answer_keys, answer_values, prompt_keys, prompt_values)
    far = shifted(own, 2)
    if size % 2 == 0:
        near = [
            lax.ppermute(own, "row", [(i, i + 1) for i in range(0, size, 2)]),
            lax.ppermute(far, "row", [(i + 1, i) for i in range(0, size, 2)]),
        ]
    else:
        near = [shifted(own, 1)]
    shared = lax.all_to_all(spread, "row", 0, 0, tiled=True).reshape(prompt, 2 * columns)

    k_block, v_block = key_cols(height), value_cols(height)
    near_ins = [pair for part in near for pair in ((k_block, part), (v_block, part))]
    ins = [
        (fixed(1, lengths.shape[0]), lengths.reshape(1, -1)),
        (fixed(1, height), weights.reshape(1, -1)),
        (wide, queries), (wide, out_grad), (key_cols(prompt), shared), (value_cols(prompt), shared),
        (k_block, far), (v_block, far), *near_ins, (k_block, own), (v_block, own),
    ]
    outs = [
        (wide, shape(*queries.shape)),
        (wide, shape(*queries.shape)),
        (fixed(prompt, 2 * columns), shape(prompt, 2 * columns)),
        (fixed(height, 2 * columns), shape(height, 2 * columns)),
        (fixed(height, 2 * columns), shape(height, 2 * columns)),
        (fixed(height, 2 * columns), shape(height, 2 * columns, F32)),
    ]
    attn_out, q_grad, terms, far_terms, near_terms, own_terms = pl.pallas_call(
        lambda *refs: attention_kernel(len(near), *refs),
        grid=(kv_heads,),
        in_specs=[spec for spec, _ in ins],
        out_specs=[spec for spec, _ in outs],
        out_shape=[kind for _, kind in outs],
        scratch_shapes=[
            pltpu.VMEM((PARTS, window, flat // kv_heads // PARTS), F32),
            pltpu.VMEM((height, HEAD_DIM), F32),
            pltpu.VMEM((prompt + 3 * height, HEAD_DIM), F32),
            pltpu.VMEM((prompt + 3 * height, HEAD_DIM), F32),
        ],
        compiler_params=pltpu.CompilerParams(vmem_limit_bytes=VMEM_LIMIT),
        cost_estimate=pl.CostEstimate(
            flops=12 * flat * (prompt + window) * HEAD_DIM, bytes_accessed=6_000_000, transcendentals=2_000_000
        ),
    )(*[array for _, array in ins])
    arrived = lax.all_to_all(terms.reshape(size, own_prompt, 2 * columns), "row", 0, 0, tiled=True)
    from_far, from_near = shifted(far_terms, -2), shifted(near_terms, -1)
    window_grad = (own_terms + from_near.astype(F32) + from_far.astype(F32)).astype(BF16)
    summed = jnp.sum(arrived.astype(F32), axis=0)
    return (
        attn_out, q_grad, window_grad[:, :columns], window_grad[:, columns:], summed[:, :columns], summed[:, columns:],
    )


def solution(mesh):
    rows = P(("grp", "row"), None)
    return jax.shard_map(
        per_device,
        mesh=mesh,
        in_specs=(rows,) * 6 + (P(("grp", "row")), P("grp")),
        out_specs=(rows,) * 6,
        check_vma=False,
    )
```

```python
import math

import jax
import jax.numpy as jnp
from jax import lax
from jax.experimental import pallas as pl
from jax.experimental.pallas import tpu as pltpu
from jax.sharding import PartitionSpec as P

HEAD_DIM = 128
PARTS = 4
FACTOR = HEAD_DIM**-0.5
EXPONENT = FACTOR * math.log2(math.e)
MASKED = -1e30
BF16 = jnp.bfloat16
F32 = jnp.float32
VMEM_LIMIT = 32 * 2**20
LAYOUT_GFLOP = 3
OUTPUTS_GFLOP = 5


def shifted(x, by):
    length = lax.axis_size("row")
    pairs = [(i, i + by) for i in range(length) if 0 <= i + by < length]
    return lax.ppermute(x, "row", pairs)


def from_other_core(x):
    return lax.ppermute(x, "row", [(i, i ^ 1) for i in range(lax.axis_size("row"))])


def across_chips(x):
    size = lax.axis_size("row")
    groups = [list(range(core, size, 2)) for core in range(2)]
    return lax.all_to_all(x, "row", 0, 0, tiled=True, axis_index_groups=groups)


def dot_nt(former, latter):
    return lax.dot_general(former, latter, (((1,), (1,)), ((), ())), preferred_element_type=F32)


def dot_nn(former, latter):
    return lax.dot_general(former, latter, (((1,), (0,)), ((), ())), preferred_element_type=F32)


def transposed(x):
    return x.astype(F32).T.astype(BF16)


def answer_starts(lengths_row, height, lanes):
    answers = lengths_row.shape[1]
    rows = height // PARTS
    before = lax.broadcasted_iota(jnp.int32, (answers, answers), 1) < lax.broadcasted_iota(
        jnp.int32, (answers, answers), 0
    )
    spread = jnp.broadcast_to(lengths_row.astype(F32), (answers, answers))
    starts = jnp.sum(jnp.where(before, spread, 0.0), axis=1, keepdims=True)
    first = lax.axis_index("row") * height
    lane = lax.rem(lax.broadcasted_iota(jnp.int32, (1, lanes), 1), rows)
    found = []
    for part in range(PARTS):
        own = (lane + (first + part * rows)).astype(F32)
        begin = jnp.max(jnp.where(starts <= own, starts, 0.0), axis=0, keepdims=True)
        found.append(begin - (first + part * rows).astype(F32))
    return found


def window_bias(begin, window, rows):
    shape = (window, begin.shape[1])
    key = (lax.broadcasted_iota(jnp.int32, shape, 0) - (window - rows)).astype(F32)
    own = lax.rem(lax.broadcasted_iota(jnp.int32, (1, begin.shape[1]), 1), rows).astype(F32)
    return jnp.where((key <= own) & (key >= begin), 0.0, MASKED)


def staged(*stages):
    held = {}
    for step in range(PARTS + len(stages) - 1):
        for place, stage in enumerate(stages):
            part = step - place
            if 0 <= part < PARTS:
                held[part] = stage(part, held.get(part))


def for_heads(count, body):
    def step(g, carry):
        body(g)
        return carry

    lax.fori_loop(0, count, step, 0)


def columns_of(g, width=HEAD_DIM):
    return pl.ds(pl.multiple_of(g * width, width), width)


def stack(refs, cols):
    return jnp.concatenate([ref[:, cols] for ref in refs], axis=0)


def pack_kernel(k_ref, v_ref, pk_ref, pv_ref, own_ref, spread_ref):
    own_ref[...] = jnp.concatenate([k_ref[...], v_ref[...]], axis=1)
    pair = jnp.concatenate([pk_ref[...], pv_ref[...]], axis=1)
    spread_ref[...] = jnp.broadcast_to(pair[None], spread_ref.shape)


def layout_kernel(
    lengths_hbm, weights_hbm, q_hbm, do_hbm, qf_ref, cot_hbm, begin_ref,
    lengths_ref, weights_ref, q_ref, do_ref, cot_ref, small_sems, in_sems, out_sems,
):
    height = q_ref.shape[1]
    kv_heads = q_ref.shape[0]
    heads = q_ref.shape[2] // HEAD_DIM
    rows = height // PARTS
    small = [
        pltpu.make_async_copy(lengths_hbm, lengths_ref, small_sems.at[0]),
        pltpu.make_async_copy(weights_hbm, weights_ref, small_sems.at[1]),
    ]
    arriving = []
    for g in range(kv_heads):
        cols = pl.ds(g * heads * HEAD_DIM, heads * HEAD_DIM)
        arriving.append(pltpu.make_async_copy(do_hbm.at[:, cols], do_ref.at[g], in_sems.at[1, g]))
        arriving.append(pltpu.make_async_copy(q_hbm.at[:, cols], q_ref.at[g], in_sems.at[0, g]))
    for copy in small + arriving:
        copy.start()
    for copy in small:
        copy.wait()
    for part, begin in enumerate(answer_starts(lengths_ref[...], height, heads * rows)):
        begin_ref[part, 0:1] = begin
    spread = jnp.broadcast_to(weights_ref[...], (HEAD_DIM, height)).T
    leaving = []
    for g in range(kv_heads):
        arriving[2 * g].wait()
        arriving[2 * g + 1].wait()
        for part in range(PARTS):
            at = slice(part * rows, (part + 1) * rows)
            for h in range(heads):
                cols = slice(h * HEAD_DIM, (h + 1) * HEAD_DIM)
                to = slice(h * rows, (h + 1) * rows)
                cot_ref[g, part, to] = (do_ref[g, at, cols].astype(F32) * spread[at]).astype(BF16)
                qf_ref[g, part, to] = q_ref[g, at, cols]
        leaving.append(pltpu.make_async_copy(cot_ref.at[g], cot_hbm.at[g], out_sems.at[g]))
        leaving[-1].start()
    for copy in leaving:
        copy.wait()


def window_kernel(
    qf_ref, cot_hbm, begin_ref, far_ref, near_ref, own_ref,
    cot_ref, powers_ref, slopes_ref, stats_ref, bias_ref, sems,
):
    kv_heads = qf_ref.shape[0]
    window = powers_ref.shape[2]
    rows = far_ref.shape[0] // PARTS

    def arrival(g):
        return pltpu.make_async_copy(cot_hbm.at[g], cot_ref.at[g], sems.at[g])

    for g in range(kv_heads):
        arrival(g).start()
    for part in range(PARTS):
        bias_ref[part] = window_bias(begin_ref[part, 0:1], window, rows)

    def head(g):
        arrival(g).wait()
        keys = stack((far_ref, near_ref, own_ref), columns_of(g))
        values = stack((far_ref, near_ref, own_ref), columns_of(g + kv_heads))

        def score(part, _):
            at = slice(part * rows, part * rows + window)
            return dot_nt(keys[at], qf_ref[g, part]), dot_nt(values[at], cot_ref[g, part])

        def weigh(part, held):
            scores, slopes = held
            scores = scores + bias_ref[part]
            highest = jnp.max(scores, axis=0, keepdims=True)
            powers = jnp.exp2((scores - highest) * EXPONENT)
            powers_ref[g, part] = powers
            slopes_ref[g, part] = slopes
            stats_ref[g, part, 0:1] = highest
            stats_ref[g, part, 1:2] = jnp.sum(powers, axis=0, keepdims=True)
            stats_ref[g, part, 2:3] = jnp.sum(powers * slopes, axis=0, keepdims=True)

        staged(score, weigh)

    for_heads(kv_heads, head)


def terms_kernel(
    qf_ref, cot_ref, powers_ref, slopes_ref, stats_ref, same_ref, other_ref,
    keep_ref, pass_ref, far_ref, own_ref, chances_hbm, grad_hbm, chances_ref, grad_ref, dk_ref, dv_ref, sems,
):
    kv_heads = qf_ref.shape[0]
    window = powers_ref.shape[2]
    half = same_ref.shape[0]
    prompt = 2 * half
    height = far_ref.shape[0]
    rows = height // PARTS

    def copies(g, part):
        return (
            pltpu.make_async_copy(chances_ref.at[g, part], chances_hbm.at[g, part], sems.at[0, g, part]),
            pltpu.make_async_copy(grad_ref.at[g, part], grad_hbm.at[g, part], sems.at[1, g, part]),
        )

    def head(g):
        keys = stack((same_ref, other_ref), columns_of(g))
        values = stack((same_ref, other_ref), columns_of(g + kv_heads))
        dk_ref[...] = jnp.zeros_like(dk_ref)
        dv_ref[...] = jnp.zeros_like(dv_ref)

        def score(part, _):
            return dot_nt(keys, qf_ref[g, part]), dot_nt(values, cot_ref[g, part])

        def weigh(part, held):
            scores, slopes = held
            window_high, window_sum, window_delta = (stats_ref[g, part, i : i + 1] for i in range(3))
            highest = jnp.maximum(jnp.max(scores, axis=0, keepdims=True), window_high)
            powers = jnp.exp2((scores - highest) * EXPONENT)
            fade = jnp.exp2((window_high - highest) * EXPONENT)
            inverse = 1.0 / (jnp.sum(powers, axis=0, keepdims=True) + fade * window_sum)
            scale = fade * inverse
            chances = powers * inverse
            delta = jnp.sum(chances * slopes, axis=0, keepdims=True) + scale * window_delta
            chances_ref[g, part, :prompt] = chances.astype(BF16)
            grad_ref[g, part, :prompt] = (chances * (slopes - delta)).astype(BF16)
            chances = powers_ref[g, part] * scale
            chances_ref[g, part, prompt:] = chances.astype(BF16)
            grad_ref[g, part, prompt:] = (chances * (slopes_ref[g, part] - delta)).astype(BF16)

        def gather(part, _):
            for copy in copies(g, part):
                copy.start()
            begin = prompt + part * rows
            for ref, former, latter in ((dk_ref, grad_ref, qf_ref), (dv_ref, chances_ref, cot_ref)):
                terms = dot_nn(former[g, part], latter[g, part])
                ref[:prompt] += terms[:prompt]
                ref[begin : begin + window] += terms[prompt:]

        staged(score, weigh, gather)
        far, near, own = (slice(prompt + i * height, prompt + (i + 1) * height) for i in range(3))
        for ref, into, source in (
            (keep_ref, slice(0, half), slice(0, half)),
            (pass_ref, slice(0, half), slice(half, prompt)),
            (pass_ref, slice(half, half + height), near),
            (far_ref, slice(0, height), far),
            (own_ref, slice(0, height), own),
        ):
            ref[into, columns_of(g)] = (dk_ref[source] * FACTOR).astype(ref.dtype)
            ref[into, columns_of(g + kv_heads)] = dv_ref[source].astype(ref.dtype)

    for_heads(kv_heads, head)
    for g in range(kv_heads):
        for part in range(PARTS):
            for copy in copies(g, part):
                copy.wait()


def outputs_kernel(
    chances_hbm, grad_hbm, same_ref, other_ref, far_ref, near_ref, own_ref, out_hbm, dq_hbm,
    out_ref, dq_ref, chances_ref, grad_ref, sems, in_sems,
):
    kv_heads = chances_hbm.shape[0]
    height = far_ref.shape[0]
    prompt = 2 * same_ref.shape[0]
    rows = height // PARTS
    heads = out_ref.shape[2] // HEAD_DIM
    refs = (same_ref, other_ref, far_ref, near_ref, own_ref)

    def everywhere(x, part):
        before, after = part * rows, height - (part + 1) * rows
        pieces = [x[:prompt], jnp.zeros((before, x.shape[1]), x.dtype), x[prompt:], jnp.zeros((after, x.shape[1]), x.dtype)]
        return jnp.concatenate([piece for piece in pieces if piece.shape[0]], axis=0)

    def copies(g):
        cols = columns_of(g, heads * HEAD_DIM)
        return (
            pltpu.make_async_copy(out_ref.at[g], out_hbm.at[:, cols], sems.at[0, g]),
            pltpu.make_async_copy(dq_ref.at[g], dq_hbm.at[:, cols], sems.at[1, g]),
        )

    def arrivals(g):
        return (
            pltpu.make_async_copy(chances_hbm.at[g], chances_ref.at[g], in_sems.at[0, g]),
            pltpu.make_async_copy(grad_hbm.at[g], grad_ref.at[g], in_sems.at[1, g]),
        )

    for g in range(kv_heads):
        for copy in arrivals(g):
            copy.start()

    def head(g):
        for copy in arrivals(g):
            copy.wait()
        keys_t = transposed(stack(refs, columns_of(g)))
        values_t = transposed(stack(refs, columns_of(g + kv_heads)))

        def multiply(part, _):
            out = dot_nn(values_t, everywhere(chances_ref[g, part], part))
            return out, dot_nn(keys_t, everywhere(grad_ref[g, part], part)) * FACTOR

        def turn(part, held):
            for ref, value in zip((out_ref, dq_ref), held):
                value = value.T.astype(BF16)
                for h in range(heads):
                    at = slice(part * rows, (part + 1) * rows)
                    ref[g, at, h * HEAD_DIM : (h + 1) * HEAD_DIM] = value[h * rows : (h + 1) * rows]

        staged(multiply, turn)
        for copy in copies(g):
            copy.start()

    for_heads(kv_heads, head)
    for g in range(kv_heads):
        for copy in copies(g):
            copy.wait()


def sums_kernel(
    own_ref, passed_ref, far_ref, arrived_ref, ak_hbm, av_hbm, pk_hbm, pv_hbm, ak_ref, av_ref, pk_ref, pv_ref, sems
):
    height, columns = ak_ref.shape
    total = arrived_ref[0].astype(F32)
    for chip in range(1, arrived_ref.shape[0]):
        total += arrived_ref[chip].astype(F32)
    pk_ref[...] = total[:, :columns]
    pv_ref[...] = total[:, columns:]
    copies = [pltpu.make_async_copy(pk_ref, pk_hbm, sems.at[0]), pltpu.make_async_copy(pv_ref, pv_hbm, sems.at[1])]
    for copy in copies:
        copy.start()
    even = 1.0 - lax.rem(lax.axis_index("row"), 2).astype(F32)
    near = passed_ref[passed_ref.shape[0] - height :].astype(F32) * even
    answers = (own_ref[...] + near + far_ref[...].astype(F32)).astype(BF16)
    ak_ref[...] = answers[:, :columns]
    av_ref[...] = answers[:, columns:]
    copies += [pltpu.make_async_copy(ak_ref, ak_hbm, sems.at[2]), pltpu.make_async_copy(av_ref, av_hbm, sems.at[3])]
    for copy in copies[2:]:
        copy.start()
    for copy in copies:
        copy.wait()


def per_device(
    queries, answer_keys, answer_values, prompt_keys, prompt_values, out_grad, weights, lengths
):
    height = queries.shape[0]
    columns = answer_keys.shape[1]
    kv_heads = columns // HEAD_DIM
    span = queries.shape[1] // kv_heads
    size = lax.axis_size("row")
    own_prompt = prompt_keys.shape[0]
    half = own_prompt * size // 2
    prompt = 2 * half
    window = 2 * height + height // PARTS
    lanes = span // HEAD_DIM * height // PARTS
    parts = (kv_heads, PARTS)

    def call(kernel, outs, gflop, arrays, in_specs=None, out_specs=None, scratch=()):
        given = {} if in_specs is None else {"in_specs": in_specs}
        if out_specs is not None:
            given["out_specs"] = out_specs
        return pl.pallas_call(
            kernel,
            out_shape=outs,
            scratch_shapes=list(scratch),
            compiler_params=pltpu.CompilerParams(vmem_limit_bytes=VMEM_LIMIT),
            cost_estimate=pl.CostEstimate(flops=int(gflop * 1e9), bytes_accessed=1_000_000, transcendentals=500_000),
            **given,
        )(*arrays)

    anywhere = pl.BlockSpec(memory_space=pl.ANY)
    vmem = pl.BlockSpec(memory_space=pltpu.VMEM)

    own, spread = pl.pallas_call(
        pack_kernel,
        out_shape=[
            jax.ShapeDtypeStruct((height, 2 * columns), BF16),
            jax.ShapeDtypeStruct((size // 2, own_prompt, 2 * columns), BF16),
        ],
    )(answer_keys, answer_values, prompt_keys, prompt_values)
    far = shifted(own, 2)
    odd = lax.rem(lax.axis_index("row"), 2) == 1
    near = from_other_core(jnp.where(odd, far, own))
    same = across_chips(spread).reshape(half, 2 * columns)
    near, same = lax.optimization_barrier((near, same))
    other = from_other_core(same)

    def in_hbm(*arrays):
        return [pltpu.with_memory_space_constraint(array, pltpu.HBM) for array in arrays]

    flat_queries, cotangent, begin = call(
        layout_kernel,
        [
            pltpu.VMEM((*parts, lanes, HEAD_DIM), BF16),
            pltpu.HBM((*parts, lanes, HEAD_DIM), BF16),
            pltpu.VMEM((PARTS, 8, lanes), F32),
        ],
        LAYOUT_GFLOP,
        in_hbm(lengths.reshape(1, -1), weights.reshape(1, -1), queries, out_grad),
        in_specs=[anywhere] * 4,
        out_specs=[vmem, anywhere, vmem],
        scratch=[
            pltpu.VMEM((1, lengths.shape[0]), jnp.int32),
            pltpu.VMEM((1, height), F32),
            pltpu.VMEM((kv_heads, height, span), BF16),
            pltpu.VMEM((kv_heads, height, span), BF16),
            pltpu.VMEM((*parts, lanes, HEAD_DIM), BF16),
            pltpu.SemaphoreType.DMA((2,)),
            pltpu.SemaphoreType.DMA((2, kv_heads)),
            pltpu.SemaphoreType.DMA((kv_heads,)),
        ],
    )
    cotangent, powers, slopes, stats = call(
        window_kernel,
        [
            pltpu.VMEM((*parts, lanes, HEAD_DIM), BF16),
            pltpu.VMEM((*parts, window, lanes), F32),
            pltpu.VMEM((*parts, window, lanes), F32),
            pltpu.VMEM((*parts, 8, lanes), F32),
        ],
        3,
        [flat_queries, *in_hbm(cotangent), begin, far, near, own],
        in_specs=[vmem, anywhere] + [vmem] * 4,
        scratch=[pltpu.VMEM((PARTS, window, lanes), F32), pltpu.SemaphoreType.DMA((kv_heads,))],
    )
    keep, passed, far_terms, own_terms, chances, score_grad = call(
        terms_kernel,
        [
            pltpu.VMEM((half, 2 * columns), F32),
            pltpu.VMEM((half + height, 2 * columns), BF16),
            pltpu.VMEM((height, 2 * columns), BF16),
            pltpu.VMEM((height, 2 * columns), F32),
            pltpu.HBM((*parts, prompt + window, lanes), BF16),
            pltpu.HBM((*parts, prompt + window, lanes), BF16),
        ],
        4,
        [flat_queries, cotangent, powers, slopes, stats, same, other],
        out_specs=[vmem] * 4 + [anywhere] * 2,
        scratch=[pltpu.VMEM((*parts, prompt + window, lanes), BF16)] * 2
        + [pltpu.VMEM((prompt + 3 * height, HEAD_DIM), F32)] * 2
        + [pltpu.SemaphoreType.DMA((2, *parts))],
    )
    whole = jax.ShapeDtypeStruct(queries.shape, BF16)
    attn_out, q_grad = call(
        outputs_kernel,
        [whole, whole],
        OUTPUTS_GFLOP,
        [*in_hbm(chances, score_grad), same, other, far, near, own],
        in_specs=[anywhere] * 2 + [vmem] * 5,
        out_specs=[anywhere, anywhere],
        scratch=[pltpu.VMEM((kv_heads, height, span), BF16)] * 2
        + [pltpu.VMEM((*parts, prompt + window, lanes), BF16)] * 2
        + [pltpu.SemaphoreType.DMA((2, kv_heads))] * 2,
    )
    passed = from_other_core(passed)
    both = (keep + passed[:half].astype(F32)).astype(BF16)
    far_terms = (far_terms.astype(F32) + jnp.where(odd, passed[half:].astype(F32), 0.0)).astype(BF16)
    both, far_terms = lax.optimization_barrier((both, far_terms))
    from_far = shifted(far_terms, -2)
    arrived = across_chips(both.reshape(size // 2, own_prompt, 2 * columns))
    answer_grad = jax.ShapeDtypeStruct((height, columns), BF16)
    prompt_grad = jax.ShapeDtypeStruct((own_prompt, columns), F32)
    dk, dv, dpk, dpv = call(
        sums_kernel,
        [answer_grad, answer_grad, prompt_grad, prompt_grad],
        0.1,
        [own_terms, passed, from_far, arrived],
        out_specs=[anywhere] * 4,
        scratch=[pltpu.VMEM((height, columns), BF16)] * 2
        + [pltpu.VMEM((own_prompt, columns), F32)] * 2
        + [pltpu.SemaphoreType.DMA((4,))],
    )
    return attn_out, q_grad, dk, dv, dpk, dpv


def solution(mesh):
    rows = P(("grp", "row"), None)
    return jax.shard_map(
        per_device,
        mesh=mesh,
        in_specs=(rows,) * 6 + (P(("grp", "row")), P("grp")),
        out_specs=(rows,) * 6,
        check_vma=False,
    )
```

```python
import math

import jax
import jax.numpy as jnp
from jax import lax
from jax.experimental import pallas as pl
from jax.experimental.pallas import tpu as pltpu
from jax.sharding import PartitionSpec as P

HEAD_DIM = 128
PARTS = 4
FACTOR = HEAD_DIM**-0.5
EXPONENT = FACTOR * math.log2(math.e)
MASKED = -1e30
BF16 = jnp.bfloat16
F32 = jnp.float32
VMEM_LIMIT = 32 * 2**20
LAYOUT_GFLOP = 3
OUTPUTS_GFLOP = 5


def shifted(x, by):
    length = lax.axis_size("row")
    pairs = [(i, i + by) for i in range(length) if 0 <= i + by < length]
    return lax.ppermute(x, "row", pairs)


def from_other_core(x):
    return lax.ppermute(x, "row", [(i, i ^ 1) for i in range(lax.axis_size("row"))])


def across_chips(x):
    size = lax.axis_size("row")
    groups = [list(range(core, size, 2)) for core in range(2)]
    return lax.all_to_all(x, "row", 0, 0, tiled=True, axis_index_groups=groups)


def dot_nt(former, latter):
    return lax.dot_general(former, latter, (((1,), (1,)), ((), ())), preferred_element_type=F32)


def dot_nn(former, latter):
    return lax.dot_general(former, latter, (((1,), (0,)), ((), ())), preferred_element_type=F32)


def transposed(x):
    return x.astype(F32).T.astype(BF16)


def answer_starts(lengths_row, height, lanes):
    answers = lengths_row.shape[1]
    rows = height // PARTS
    before = lax.broadcasted_iota(jnp.int32, (answers, answers), 1) < lax.broadcasted_iota(
        jnp.int32, (answers, answers), 0
    )
    spread = jnp.broadcast_to(lengths_row.astype(F32), (answers, answers))
    starts = jnp.sum(jnp.where(before, spread, 0.0), axis=1, keepdims=True)
    first = lax.axis_index("row") * height
    lane = lax.rem(lax.broadcasted_iota(jnp.int32, (1, lanes), 1), rows)
    found = []
    for part in range(PARTS):
        own = (lane + (first + part * rows)).astype(F32)
        begin = jnp.max(jnp.where(starts <= own, starts, 0.0), axis=0, keepdims=True)
        found.append(begin - (first + part * rows).astype(F32))
    return found


def window_bias(begin, window, rows):
    shape = (window, begin.shape[1])
    key = (lax.broadcasted_iota(jnp.int32, shape, 0) - (window - rows)).astype(F32)
    own = lax.rem(lax.broadcasted_iota(jnp.int32, (1, begin.shape[1]), 1), rows).astype(F32)
    return jnp.where((key <= own) & (key >= begin), 0.0, MASKED)


def staged(*stages):
    held = {}
    for step in range(PARTS + len(stages) - 1):
        for place, stage in enumerate(stages):
            part = step - place
            if 0 <= part < PARTS:
                held[part] = stage(part, held.get(part))


def for_heads(count, body):
    def step(g, carry):
        body(g)
        return carry

    lax.fori_loop(0, count, step, 0)


def columns_of(g, width=HEAD_DIM):
    return pl.ds(pl.multiple_of(g * width, width), width)


def stack(refs, cols):
    return jnp.concatenate([ref[:, cols] for ref in refs], axis=0)


def pack_kernel(k_ref, v_ref, pk_ref, pv_ref, own_ref, spread_ref):
    own_ref[...] = jnp.concatenate([k_ref[...], v_ref[...]], axis=1)
    pair = jnp.concatenate([pk_ref[...], pv_ref[...]], axis=1)
    spread_ref[...] = jnp.broadcast_to(pair[None], spread_ref.shape)


def layout_kernel(
    lengths_hbm, weights_hbm, q_hbm, do_hbm, qf_ref, cot_hbm, begin_ref,
    lengths_ref, weights_ref, q_ref, do_ref, cot_ref, small_sems, in_sems, out_sems,
):
    height = q_ref.shape[1]
    kv_heads = q_ref.shape[0]
    heads = q_ref.shape[2] // HEAD_DIM
    rows = height // PARTS
    small = [
        pltpu.make_async_copy(lengths_hbm, lengths_ref, small_sems.at[0]),
        pltpu.make_async_copy(weights_hbm, weights_ref, small_sems.at[1]),
    ]
    arriving = []
    for g in range(kv_heads):
        cols = pl.ds(g * heads * HEAD_DIM, heads * HEAD_DIM)
        arriving.append(pltpu.make_async_copy(do_hbm.at[:, cols], do_ref.at[g], in_sems.at[1, g]))
        arriving.append(pltpu.make_async_copy(q_hbm.at[:, cols], q_ref.at[g], in_sems.at[0, g]))
    for copy in small + arriving:
        copy.start()
    for copy in small:
        copy.wait()
    for part, begin in enumerate(answer_starts(lengths_ref[...], height, heads * rows)):
        begin_ref[part, 0:1] = begin
    spread = jnp.broadcast_to(weights_ref[...], (HEAD_DIM, height)).T
    leaving = []
    for g in range(kv_heads):
        arriving[2 * g].wait()
        arriving[2 * g + 1].wait()
        for part in range(PARTS):
            at = slice(part * rows, (part + 1) * rows)
            for h in range(heads):
                cols = slice(h * HEAD_DIM, (h + 1) * HEAD_DIM)
                to = slice(h * rows, (h + 1) * rows)
                cot_ref[g, part, to] = (do_ref[g, at, cols].astype(F32) * spread[at]).astype(BF16)
                qf_ref[g, part, to] = q_ref[g, at, cols]
        leaving.append(pltpu.make_async_copy(cot_ref.at[g], cot_hbm.at[g], out_sems.at[g]))
        leaving[-1].start()
    for copy in leaving:
        copy.wait()


def window_kernel(
    qf_ref, cot_hbm, begin_ref, far_ref, near_ref, own_ref,
    cot_ref, powers_ref, slopes_ref, stats_ref, bias_ref, sems,
):
    kv_heads = qf_ref.shape[0]
    window = powers_ref.shape[2]
    rows = far_ref.shape[0] // PARTS

    def arrival(g):
        return pltpu.make_async_copy(cot_hbm.at[g], cot_ref.at[g], sems.at[g])

    for g in range(kv_heads):
        arrival(g).start()
    for part in range(PARTS):
        bias_ref[part] = window_bias(begin_ref[part, 0:1], window, rows)

    def head(g):
        arrival(g).wait()
        keys = stack((far_ref, near_ref, own_ref), columns_of(g))
        values = stack((far_ref, near_ref, own_ref), columns_of(g + kv_heads))

        def score(part, _):
            at = slice(part * rows, part * rows + window)
            return dot_nt(keys[at], qf_ref[g, part]), dot_nt(values[at], cot_ref[g, part])

        def weigh(part, held):
            scores, slopes = held
            scores = scores + bias_ref[part]
            highest = jnp.max(scores, axis=0, keepdims=True)
            powers = jnp.exp2((scores - highest) * EXPONENT)
            powers_ref[g, part] = powers
            slopes_ref[g, part] = slopes
            stats_ref[g, part, 0:1] = highest
            stats_ref[g, part, 1:2] = jnp.sum(powers, axis=0, keepdims=True)
            stats_ref[g, part, 2:3] = jnp.sum(powers * slopes, axis=0, keepdims=True)

        staged(score, weigh)

    for_heads(kv_heads, head)


def terms_kernel(
    qf_ref, cot_ref, powers_ref, slopes_ref, stats_ref, same_ref, other_ref,
    keep_ref, pass_ref, near_ref, far_ref, own_ref, chances_hbm, grad_hbm, chances_ref, grad_ref, dk_ref, dv_ref, sems,
):
    kv_heads = qf_ref.shape[0]
    window = powers_ref.shape[2]
    half = same_ref.shape[0]
    prompt = 2 * half
    height = far_ref.shape[0]
    rows = height // PARTS

    def copies(g):
        return (
            pltpu.make_async_copy(chances_ref.at[g], chances_hbm.at[g], sems.at[0, g]),
            pltpu.make_async_copy(grad_ref.at[g], grad_hbm.at[g], sems.at[1, g]),
        )

    def head(g):
        keys = stack((same_ref, other_ref), columns_of(g))
        values = stack((same_ref, other_ref), columns_of(g + kv_heads))
        dk_ref[...] = jnp.zeros_like(dk_ref)
        dv_ref[...] = jnp.zeros_like(dv_ref)

        def score(part, _):
            return dot_nt(keys, qf_ref[g, part]), dot_nt(values, cot_ref[g, part])

        def weigh(part, held):
            scores, slopes = held
            window_high, window_sum, window_delta = (stats_ref[g, part, i : i + 1] for i in range(3))
            highest = jnp.maximum(jnp.max(scores, axis=0, keepdims=True), window_high)
            powers = jnp.exp2((scores - highest) * EXPONENT)
            fade = jnp.exp2((window_high - highest) * EXPONENT)
            inverse = 1.0 / (jnp.sum(powers, axis=0, keepdims=True) + fade * window_sum)
            scale = fade * inverse
            chances = powers * inverse
            delta = jnp.sum(chances * slopes, axis=0, keepdims=True) + scale * window_delta
            chances_ref[g, part, :prompt] = chances.astype(BF16)
            grad_ref[g, part, :prompt] = (chances * (slopes - delta)).astype(BF16)
            chances = powers_ref[g, part] * scale
            chances_ref[g, part, prompt:] = chances.astype(BF16)
            grad_ref[g, part, prompt:] = (chances * (slopes_ref[g, part] - delta)).astype(BF16)

        def gather(part, _):
            begin = prompt + part * rows
            for ref, former, latter in ((dk_ref, grad_ref, qf_ref), (dv_ref, chances_ref, cot_ref)):
                terms = dot_nn(former[g, part], latter[g, part])
                ref[:prompt] += terms[:prompt]
                ref[begin : begin + window] += terms[prompt:]

        staged(score, weigh, gather)
        for copy in copies(g):
            copy.start()
        far, near, own = (slice(prompt + i * height, prompt + (i + 1) * height) for i in range(3))
        for ref, into, source in (
            (keep_ref, slice(0, half), slice(0, half)),
            (pass_ref, slice(0, half), slice(half, prompt)),
            (near_ref, slice(0, height), near),
            (far_ref, slice(0, height), far),
            (own_ref, slice(0, height), own),
        ):
            ref[into, columns_of(g)] = (dk_ref[source] * FACTOR).astype(ref.dtype)
            ref[into, columns_of(g + kv_heads)] = dv_ref[source].astype(ref.dtype)

    for_heads(kv_heads, head)
    for g in range(kv_heads):
        for copy in copies(g):
            copy.wait()


def outputs_kernel(
    chances_hbm, grad_hbm, same_ref, other_ref, far_ref, near_ref, own_ref, out_hbm, dq_hbm,
    out_ref, dq_ref, chances_ref, grad_ref, sems, in_sems,
):
    kv_heads = chances_hbm.shape[0]
    height = far_ref.shape[0]
    prompt = 2 * same_ref.shape[0]
    rows = height // PARTS
    heads = out_ref.shape[2] // HEAD_DIM
    refs = (same_ref, other_ref, far_ref, near_ref, own_ref)

    def everywhere(x, part):
        before, after = part * rows, height - (part + 1) * rows
        pieces = [x[:prompt], jnp.zeros((before, x.shape[1]), x.dtype), x[prompt:], jnp.zeros((after, x.shape[1]), x.dtype)]
        return jnp.concatenate([piece for piece in pieces if piece.shape[0]], axis=0)

    def copies(g):
        cols = columns_of(g, heads * HEAD_DIM)
        return (
            pltpu.make_async_copy(out_ref.at[g], out_hbm.at[:, cols], sems.at[0, g]),
            pltpu.make_async_copy(dq_ref.at[g], dq_hbm.at[:, cols], sems.at[1, g]),
        )

    def arrivals(g):
        return (
            pltpu.make_async_copy(chances_hbm.at[g], chances_ref.at[g], in_sems.at[0, g]),
            pltpu.make_async_copy(grad_hbm.at[g], grad_ref.at[g], in_sems.at[1, g]),
        )

    for g in range(kv_heads):
        for copy in arrivals(g):
            copy.start()

    def head(g):
        for copy in arrivals(g):
            copy.wait()
        keys_t = transposed(stack(refs, columns_of(g)))
        values_t = transposed(stack(refs, columns_of(g + kv_heads)))

        def multiply(part, _):
            out = dot_nn(values_t, everywhere(chances_ref[g, part], part))
            return out, dot_nn(keys_t, everywhere(grad_ref[g, part], part)) * FACTOR

        def turn(part, held):
            for ref, value in zip((out_ref, dq_ref), held):
                value = value.T.astype(BF16)
                for h in range(heads):
                    at = slice(part * rows, (part + 1) * rows)
                    ref[g, at, h * HEAD_DIM : (h + 1) * HEAD_DIM] = value[h * rows : (h + 1) * rows]

        staged(multiply, turn)
        for copy in copies(g):
            copy.start()

    for_heads(kv_heads, head)
    for g in range(kv_heads):
        for copy in copies(g):
            copy.wait()


def sums_kernel(
    own_ref, near_ref, far_ref, arrived_ref, ak_hbm, av_hbm, pk_hbm, pv_hbm, ak_ref, av_ref, pk_ref, pv_ref, sems
):
    height, columns = ak_ref.shape
    total = arrived_ref[0].astype(F32)
    for chip in range(1, arrived_ref.shape[0]):
        total += arrived_ref[chip].astype(F32)
    pk_ref[...] = total[:, :columns]
    pv_ref[...] = total[:, columns:]
    copies = [pltpu.make_async_copy(pk_ref, pk_hbm, sems.at[0]), pltpu.make_async_copy(pv_ref, pv_hbm, sems.at[1])]
    for copy in copies:
        copy.start()
    even = 1.0 - lax.rem(lax.axis_index("row"), 2).astype(F32)
    near = near_ref[...].astype(F32) * even
    answers = (own_ref[...] + near + far_ref[...].astype(F32)).astype(BF16)
    ak_ref[...] = answers[:, :columns]
    av_ref[...] = answers[:, columns:]
    copies += [pltpu.make_async_copy(ak_ref, ak_hbm, sems.at[2]), pltpu.make_async_copy(av_ref, av_hbm, sems.at[3])]
    for copy in copies[2:]:
        copy.start()
    for copy in copies:
        copy.wait()


def per_device(
    queries, answer_keys, answer_values, prompt_keys, prompt_values, out_grad, weights, lengths
):
    height = queries.shape[0]
    columns = answer_keys.shape[1]
    kv_heads = columns // HEAD_DIM
    span = queries.shape[1] // kv_heads
    size = lax.axis_size("row")
    own_prompt = prompt_keys.shape[0]
    half = own_prompt * size // 2
    prompt = 2 * half
    window = 2 * height + height // PARTS
    lanes = span // HEAD_DIM * height // PARTS
    parts = (kv_heads, PARTS)

    def call(kernel, outs, gflop, arrays, in_specs=None, out_specs=None, scratch=()):
        given = {} if in_specs is None else {"in_specs": in_specs}
        if out_specs is not None:
            given["out_specs"] = out_specs
        return pl.pallas_call(
            kernel,
            out_shape=outs,
            scratch_shapes=list(scratch),
            compiler_params=pltpu.CompilerParams(vmem_limit_bytes=VMEM_LIMIT),
            cost_estimate=pl.CostEstimate(flops=int(gflop * 1e9), bytes_accessed=1_000_000, transcendentals=500_000),
            **given,
        )(*arrays)

    anywhere = pl.BlockSpec(memory_space=pl.ANY)
    vmem = pl.BlockSpec(memory_space=pltpu.VMEM)

    own, spread = pl.pallas_call(
        pack_kernel,
        out_shape=[
            pltpu.VMEM((height, 2 * columns), BF16),
            jax.ShapeDtypeStruct((size // 2, own_prompt, 2 * columns), BF16),
        ],
    )(answer_keys, answer_values, prompt_keys, prompt_values)
    far = shifted(own, 2)
    odd = lax.rem(lax.axis_index("row"), 2) == 1
    near = from_other_core(jnp.where(odd, far, own))
    same = across_chips(spread).reshape(half, 2 * columns)
    near, same = lax.optimization_barrier((near, same))
    other = from_other_core(same)

    def in_hbm(*arrays):
        return [pltpu.with_memory_space_constraint(array, pltpu.HBM) for array in arrays]

    flat_queries, cotangent, begin = call(
        layout_kernel,
        [
            pltpu.VMEM((*parts, lanes, HEAD_DIM), BF16),
            pltpu.HBM((*parts, lanes, HEAD_DIM), BF16),
            pltpu.VMEM((PARTS, 8, lanes), F32),
        ],
        LAYOUT_GFLOP,
        in_hbm(lengths.reshape(1, -1), weights.reshape(1, -1), queries, out_grad),
        in_specs=[anywhere] * 4,
        out_specs=[vmem, anywhere, vmem],
        scratch=[
            pltpu.VMEM((1, lengths.shape[0]), jnp.int32),
            pltpu.VMEM((1, height), F32),
            pltpu.VMEM((kv_heads, height, span), BF16),
            pltpu.VMEM((kv_heads, height, span), BF16),
            pltpu.VMEM((*parts, lanes, HEAD_DIM), BF16),
            pltpu.SemaphoreType.DMA((2,)),
            pltpu.SemaphoreType.DMA((2, kv_heads)),
            pltpu.SemaphoreType.DMA((kv_heads,)),
        ],
    )
    cotangent, powers, slopes, stats = call(
        window_kernel,
        [
            pltpu.VMEM((*parts, lanes, HEAD_DIM), BF16),
            pltpu.VMEM((*parts, window, lanes), F32),
            pltpu.VMEM((*parts, window, lanes), F32),
            pltpu.VMEM((*parts, 8, lanes), F32),
        ],
        3,
        [flat_queries, *in_hbm(cotangent), begin, far, near, own],
        in_specs=[vmem, anywhere] + [vmem] * 4,
        scratch=[pltpu.VMEM((PARTS, window, lanes), F32), pltpu.SemaphoreType.DMA((kv_heads,))],
    )
    keep, passed, near_terms, far_terms, own_terms, chances, score_grad = call(
        terms_kernel,
        [
            pltpu.VMEM((half, 2 * columns), F32),
            pltpu.VMEM((half, 2 * columns), BF16),
            pltpu.VMEM((height, 2 * columns), BF16),
            pltpu.VMEM((height, 2 * columns), BF16),
            pltpu.VMEM((height, 2 * columns), F32),
            pltpu.HBM((*parts, prompt + window, lanes), BF16),
            pltpu.HBM((*parts, prompt + window, lanes), BF16),
        ],
        4,
        [flat_queries, cotangent, powers, slopes, stats, same, other],
        out_specs=[vmem] * 5 + [anywhere] * 2,
        scratch=[pltpu.VMEM((*parts, prompt + window, lanes), BF16)] * 2
        + [pltpu.VMEM((prompt + 3 * height, HEAD_DIM), F32)] * 2
        + [pltpu.SemaphoreType.DMA((2, kv_heads))],
    )
    whole = jax.ShapeDtypeStruct(queries.shape, BF16)
    attn_out, q_grad = call(
        outputs_kernel,
        [whole, whole],
        OUTPUTS_GFLOP,
        [*in_hbm(chances, score_grad), same, other, far, near, own],
        in_specs=[anywhere] * 2 + [vmem] * 5,
        out_specs=[anywhere, anywhere],
        scratch=[pltpu.VMEM((kv_heads, height, span), BF16)] * 2
        + [pltpu.VMEM((*parts, prompt + window, lanes), BF16)] * 2
        + [pltpu.SemaphoreType.DMA((2, kv_heads))] * 2,
    )
    near_terms = from_other_core(near_terms)
    far_terms = (far_terms.astype(F32) + jnp.where(odd, near_terms.astype(F32), 0.0)).astype(BF16)
    passed, far_terms = lax.optimization_barrier((passed, far_terms))
    both = (keep + from_other_core(passed).astype(F32)).astype(BF16)
    from_far = shifted(far_terms, -2)
    arrived = across_chips(both.reshape(size // 2, own_prompt, 2 * columns))
    answer_grad = jax.ShapeDtypeStruct((height, columns), BF16)
    prompt_grad = jax.ShapeDtypeStruct((own_prompt, columns), F32)
    dk, dv, dpk, dpv = call(
        sums_kernel,
        [answer_grad, answer_grad, prompt_grad, prompt_grad],
        0.1,
        [own_terms, near_terms, from_far, arrived],
        out_specs=[anywhere] * 4,
        scratch=[pltpu.VMEM((height, columns), BF16)] * 2
        + [pltpu.VMEM((own_prompt, columns), F32)] * 2
        + [pltpu.SemaphoreType.DMA((4,))],
    )
    return attn_out, q_grad, dk, dv, dpk, dpv


def solution(mesh):
    rows = P(("grp", "row"), None)
    return jax.shard_map(
        per_device,
        mesh=mesh,
        in_specs=(rows,) * 6 + (P(("grp", "row")), P("grp")),
        out_specs=(rows,) * 6,
        check_vma=False,
    )
```

```python
import math

import jax
import jax.numpy as jnp
from jax import lax
from jax.experimental import pallas as pl
from jax.experimental.pallas import tpu as pltpu
from jax.sharding import PartitionSpec as P

HEAD_DIM = 128
PARTS = 4
FACTOR = HEAD_DIM**-0.5
EXPONENT = FACTOR * math.log2(math.e)
MASKED = -1e30
BF16 = jnp.bfloat16
F32 = jnp.float32
VMEM_LIMIT = 32 * 2**20
LAYOUT_GFLOP = 3
OUTPUTS_GFLOP = 5
STORE_GFLOP = 1


def shifted(x, by):
    length = lax.axis_size("row")
    pairs = [(i, i + by) for i in range(length) if 0 <= i + by < length]
    return lax.ppermute(x, "row", pairs)


def from_other_core(x):
    return lax.ppermute(x, "row", [(i, i ^ 1) for i in range(lax.axis_size("row"))])


def across_chips(x):
    size = lax.axis_size("row")
    groups = [list(range(core, size, 2)) for core in range(2)]
    return lax.all_to_all(x, "row", 0, 0, tiled=True, axis_index_groups=groups)


def dot_nt(former, latter):
    return lax.dot_general(former, latter, (((1,), (1,)), ((), ())), preferred_element_type=F32)


def dot_nn(former, latter):
    return lax.dot_general(former, latter, (((1,), (0,)), ((), ())), preferred_element_type=F32)


def transposed(x):
    return x.astype(F32).T.astype(BF16)


def answer_starts(lengths_row, height, lanes):
    answers = lengths_row.shape[1]
    rows = height // PARTS
    before = lax.broadcasted_iota(jnp.int32, (answers, answers), 1) < lax.broadcasted_iota(
        jnp.int32, (answers, answers), 0
    )
    spread = jnp.broadcast_to(lengths_row.astype(F32), (answers, answers))
    starts = jnp.sum(jnp.where(before, spread, 0.0), axis=1, keepdims=True)
    first = lax.axis_index("row") * height
    lane = lax.rem(lax.broadcasted_iota(jnp.int32, (1, lanes), 1), rows)
    found = []
    for part in range(PARTS):
        own = (lane + (first + part * rows)).astype(F32)
        begin = jnp.max(jnp.where(starts <= own, starts, 0.0), axis=0, keepdims=True)
        found.append(begin - (first + part * rows).astype(F32))
    return found


def window_bias(begin, window, rows):
    shape = (window, begin.shape[1])
    key = (lax.broadcasted_iota(jnp.int32, shape, 0) - (window - rows)).astype(F32)
    own = lax.rem(lax.broadcasted_iota(jnp.int32, (1, begin.shape[1]), 1), rows).astype(F32)
    return jnp.where((key <= own) & (key >= begin), 0.0, MASKED)


def staged(*stages):
    held = {}
    for step in range(PARTS + len(stages) - 1):
        for place, stage in enumerate(stages):
            part = step - place
            if 0 <= part < PARTS:
                held[part] = stage(part, held.get(part))


def for_heads(count, body):
    def step(g, carry):
        body(g)
        return carry

    lax.fori_loop(0, count, step, 0)


def columns_of(g, width=HEAD_DIM):
    begin = g * width
    return pl.ds(begin if isinstance(begin, int) else pl.multiple_of(begin, width), width)


def stack(refs, cols):
    return jnp.concatenate([ref[:, cols] for ref in refs], axis=0)


def pack_kernel(k_ref, v_ref, pk_ref, pv_ref, own_ref, spread_ref):
    own_ref[...] = jnp.concatenate([k_ref[...], v_ref[...]], axis=1)
    pair = jnp.concatenate([pk_ref[...], pv_ref[...]], axis=1)
    spread_ref[...] = jnp.broadcast_to(pair[None], spread_ref.shape)


def layout_kernel(
    lengths_hbm, weights_hbm, q_hbm, do_hbm, qf_ref, cot_hbm, begin_ref,
    lengths_ref, weights_ref, q_ref, do_ref, cot_ref, small_sems, in_sems, out_sems,
):
    height = q_ref.shape[1]
    kv_heads = q_ref.shape[0]
    heads = q_ref.shape[2] // HEAD_DIM
    rows = height // PARTS
    small = [
        pltpu.make_async_copy(lengths_hbm, lengths_ref, small_sems.at[0]),
        pltpu.make_async_copy(weights_hbm, weights_ref, small_sems.at[1]),
    ]
    arriving = []
    for g in range(kv_heads):
        cols = pl.ds(g * heads * HEAD_DIM, heads * HEAD_DIM)
        arriving.append(pltpu.make_async_copy(do_hbm.at[:, cols], do_ref.at[g], in_sems.at[1, g]))
        arriving.append(pltpu.make_async_copy(q_hbm.at[:, cols], q_ref.at[g], in_sems.at[0, g]))
    for copy in small + arriving:
        copy.start()
    for copy in small:
        copy.wait()
    for part, begin in enumerate(answer_starts(lengths_ref[...], height, heads * rows)):
        begin_ref[part, 0:1] = begin
    spread = jnp.broadcast_to(weights_ref[...], (HEAD_DIM, height)).T
    leaving = []
    for g in range(kv_heads):
        arriving[2 * g].wait()
        arriving[2 * g + 1].wait()
        for part in range(PARTS):
            at = slice(part * rows, (part + 1) * rows)
            for h in range(heads):
                cols = slice(h * HEAD_DIM, (h + 1) * HEAD_DIM)
                to = slice(h * rows, (h + 1) * rows)
                cot_ref[g, part, to] = (do_ref[g, at, cols].astype(F32) * spread[at]).astype(BF16)
                qf_ref[g, part, to] = q_ref[g, at, cols]
        leaving.append(pltpu.make_async_copy(cot_ref.at[g], cot_hbm.at[g], out_sems.at[g]))
        leaving[-1].start()
    for copy in leaving:
        copy.wait()


def window_kernel(
    qf_ref, cot_hbm, begin_ref, far_ref, near_ref, own_ref,
    cot_ref, powers_ref, slopes_ref, stats_ref, bias_ref, sems,
):
    kv_heads = qf_ref.shape[0]
    window = powers_ref.shape[2]
    rows = far_ref.shape[0] // PARTS

    def arrival(g):
        return pltpu.make_async_copy(cot_hbm.at[g], cot_ref.at[g], sems.at[g])

    for g in range(kv_heads):
        arrival(g).start()
    for part in range(PARTS):
        bias_ref[part] = window_bias(begin_ref[part, 0:1], window, rows)

    def powers_head(g):
        keys = stack((far_ref, near_ref, own_ref), columns_of(g))

        def score(part, _):
            return dot_nt(keys[part * rows : part * rows + window], qf_ref[g, part])

        def weigh(part, scores):
            scores = scores + bias_ref[part]
            highest = jnp.max(scores, axis=0, keepdims=True)
            powers = jnp.exp2((scores - highest) * EXPONENT)
            powers_ref[g, part] = powers
            stats_ref[g, part, 0:1] = highest
            stats_ref[g, part, 1:2] = jnp.sum(powers, axis=0, keepdims=True)

        staged(score, weigh)

    def slopes_head(g):
        arrival(g).wait()
        values = stack((far_ref, near_ref, own_ref), columns_of(g + kv_heads))

        def slope(part, _):
            return dot_nt(values[part * rows : part * rows + window], cot_ref[g, part])

        def add(part, slopes):
            slopes_ref[g, part] = slopes
            stats_ref[g, part, 2:3] = jnp.sum(powers_ref[g, part] * slopes, axis=0, keepdims=True)

        staged(slope, add)

    for_heads(kv_heads, powers_head)
    for_heads(kv_heads, slopes_head)


def terms_kernel(
    qf_ref, cot_ref, powers_ref, slopes_ref, stats_ref, same_ref, other_ref,
    keep_ref, pass_ref, near_ref, far_ref, own_ref, chances_hbm, grad_hbm, last_chances_ref, last_grad_ref,
    chances_ref, grad_ref, dk_ref, dv_ref, sems,
):
    kv_heads = qf_ref.shape[0]
    window = powers_ref.shape[2]
    half = same_ref.shape[0]
    prompt = 2 * half
    height = far_ref.shape[0]
    rows = height // PARTS

    def copies(g):
        return (
            pltpu.make_async_copy(chances_ref.at[g], chances_hbm.at[g], sems.at[0, g]),
            pltpu.make_async_copy(grad_ref.at[g], grad_hbm.at[g], sems.at[1, g]),
        )

    def head(g, chances_to, grad_to):
        keys = stack((same_ref, other_ref), columns_of(g))
        values = stack((same_ref, other_ref), columns_of(g + kv_heads))
        dk_ref[...] = jnp.zeros_like(dk_ref)
        dv_ref[...] = jnp.zeros_like(dv_ref)

        def score(part, _):
            return dot_nt(keys, qf_ref[g, part]), dot_nt(values, cot_ref[g, part])

        def weigh(part, held):
            scores, slopes = held
            window_high, window_sum, window_delta = (stats_ref[g, part, i : i + 1] for i in range(3))
            highest = jnp.maximum(jnp.max(scores, axis=0, keepdims=True), window_high)
            powers = jnp.exp2((scores - highest) * EXPONENT)
            fade = jnp.exp2((window_high - highest) * EXPONENT)
            inverse = 1.0 / (jnp.sum(powers, axis=0, keepdims=True) + fade * window_sum)
            scale = fade * inverse
            chances = powers * inverse
            delta = jnp.sum(chances * slopes, axis=0, keepdims=True) + scale * window_delta
            chances_to[part, :prompt] = chances.astype(BF16)
            grad_to[part, :prompt] = (chances * (slopes - delta)).astype(BF16)
            chances = powers_ref[g, part] * scale
            chances_to[part, prompt:] = chances.astype(BF16)
            grad_to[part, prompt:] = (chances * (slopes_ref[g, part] - delta)).astype(BF16)

        def gather(part, _):
            begin = prompt + part * rows
            for ref, former, latter in ((dk_ref, grad_to, qf_ref), (dv_ref, chances_to, cot_ref)):
                terms = dot_nn(former[part], latter[g, part])
                ref[:prompt] += terms[:prompt]
                ref[begin : begin + window] += terms[prompt:]

        staged(score, weigh, gather)
        far, near, own = (slice(prompt + i * height, prompt + (i + 1) * height) for i in range(3))
        for ref, into, source in (
            (keep_ref, slice(0, half), slice(0, half)),
            (pass_ref, slice(0, half), slice(half, prompt)),
            (near_ref, slice(0, height), near),
            (far_ref, slice(0, height), far),
            (own_ref, slice(0, height), own),
        ):
            ref[into, columns_of(g)] = (dk_ref[source] * FACTOR).astype(ref.dtype)
            ref[into, columns_of(g + kv_heads)] = dv_ref[source].astype(ref.dtype)

    def stored_head(g):
        head(g, chances_ref.at[g], grad_ref.at[g])
        for copy in copies(g):
            copy.start()

    for_heads(kv_heads - 1, stored_head)
    head(kv_heads - 1, last_chances_ref, last_grad_ref)
    for g in range(kv_heads - 1):
        for copy in copies(g):
            copy.wait()


def store_kernel(chances_ref, grad_ref, chances_hbm, grad_hbm, sems):
    copies = [
        pltpu.make_async_copy(chances_ref, chances_hbm, sems.at[0]),
        pltpu.make_async_copy(grad_ref, grad_hbm, sems.at[1]),
    ]
    for copy in copies:
        copy.start()
    for copy in copies:
        copy.wait()


def outputs_kernel(
    chances_hbm, grad_hbm, last_chances_hbm, last_grad_hbm, same_ref, other_ref, far_ref, near_ref, own_ref,
    out_hbm, dq_hbm,
    out_ref, dq_ref, chances_ref, grad_ref, sems, in_sems,
):
    kv_heads = out_ref.shape[0]
    height = far_ref.shape[0]
    prompt = 2 * same_ref.shape[0]
    rows = height // PARTS
    heads = out_ref.shape[2] // HEAD_DIM
    refs = (same_ref, other_ref, far_ref, near_ref, own_ref)

    def everywhere(x, part):
        before, after = part * rows, height - (part + 1) * rows
        pieces = [x[:prompt], jnp.zeros((before, x.shape[1]), x.dtype), x[prompt:], jnp.zeros((after, x.shape[1]), x.dtype)]
        return jnp.concatenate([piece for piece in pieces if piece.shape[0]], axis=0)

    def copies(g):
        cols = columns_of(g, heads * HEAD_DIM)
        return (
            pltpu.make_async_copy(out_ref.at[g], out_hbm.at[:, cols], sems.at[0, g]),
            pltpu.make_async_copy(dq_ref.at[g], dq_hbm.at[:, cols], sems.at[1, g]),
        )

    def arrivals(g, chances_from, grad_from):
        return (
            pltpu.make_async_copy(chances_from, chances_ref.at[g], in_sems.at[0, g]),
            pltpu.make_async_copy(grad_from, grad_ref.at[g], in_sems.at[1, g]),
        )

    def stored(g):
        return arrivals(g, chances_hbm.at[g], grad_hbm.at[g])

    last = arrivals(kv_heads - 1, last_chances_hbm, last_grad_hbm)
    for g in range(kv_heads - 1):
        for copy in stored(g):
            copy.start()
    for copy in last:
        copy.start()

    def head(g, arriving):
        for copy in arriving:
            copy.wait()
        keys_t = transposed(stack(refs, columns_of(g)))
        values_t = transposed(stack(refs, columns_of(g + kv_heads)))

        def multiply(part, _):
            out = dot_nn(values_t, everywhere(chances_ref[g, part], part))
            return out, dot_nn(keys_t, everywhere(grad_ref[g, part], part)) * FACTOR

        def turn(part, held):
            for ref, value in zip((out_ref, dq_ref), held):
                value = value.T.astype(BF16)
                for h in range(heads):
                    at = slice(part * rows, (part + 1) * rows)
                    ref[g, at, h * HEAD_DIM : (h + 1) * HEAD_DIM] = value[h * rows : (h + 1) * rows]

        staged(multiply, turn)
        for copy in copies(g):
            copy.start()

    for_heads(kv_heads - 1, lambda g: head(g, stored(g)))
    head(kv_heads - 1, last)
    for g in range(kv_heads):
        for copy in copies(g):
            copy.wait()


def sums_kernel(
    own_ref, near_ref, far_ref, arrived_ref, ak_hbm, av_hbm, pk_hbm, pv_hbm, ak_ref, av_ref, pk_ref, pv_ref, sems
):
    height, columns = ak_ref.shape
    total = arrived_ref[0].astype(F32)
    for chip in range(1, arrived_ref.shape[0]):
        total += arrived_ref[chip].astype(F32)
    pk_ref[...] = total[:, :columns]
    pv_ref[...] = total[:, columns:]
    copies = [pltpu.make_async_copy(pk_ref, pk_hbm, sems.at[0]), pltpu.make_async_copy(pv_ref, pv_hbm, sems.at[1])]
    for copy in copies:
        copy.start()
    even = 1.0 - lax.rem(lax.axis_index("row"), 2).astype(F32)
    near = near_ref[...].astype(F32) * even
    answers = (own_ref[...] + near + far_ref[...].astype(F32)).astype(BF16)
    ak_ref[...] = answers[:, :columns]
    av_ref[...] = answers[:, columns:]
    copies += [pltpu.make_async_copy(ak_ref, ak_hbm, sems.at[2]), pltpu.make_async_copy(av_ref, av_hbm, sems.at[3])]
    for copy in copies[2:]:
        copy.start()
    for copy in copies:
        copy.wait()


def per_device(
    queries, answer_keys, answer_values, prompt_keys, prompt_values, out_grad, weights, lengths
):
    height = queries.shape[0]
    columns = answer_keys.shape[1]
    kv_heads = columns // HEAD_DIM
    span = queries.shape[1] // kv_heads
    size = lax.axis_size("row")
    own_prompt = prompt_keys.shape[0]
    half = own_prompt * size // 2
    prompt = 2 * half
    window = 2 * height + height // PARTS
    lanes = span // HEAD_DIM * height // PARTS
    parts = (kv_heads, PARTS)

    def call(kernel, outs, gflop, arrays, in_specs=None, out_specs=None, scratch=()):
        given = {} if in_specs is None else {"in_specs": in_specs}
        if out_specs is not None:
            given["out_specs"] = out_specs
        return pl.pallas_call(
            kernel,
            out_shape=outs,
            scratch_shapes=list(scratch),
            compiler_params=pltpu.CompilerParams(vmem_limit_bytes=VMEM_LIMIT),
            cost_estimate=pl.CostEstimate(flops=int(gflop * 1e9), bytes_accessed=1_000_000, transcendentals=500_000),
            **given,
        )(*arrays)

    anywhere = pl.BlockSpec(memory_space=pl.ANY)
    vmem = pl.BlockSpec(memory_space=pltpu.VMEM)

    own, spread = pl.pallas_call(
        pack_kernel,
        out_shape=[
            pltpu.VMEM((height, 2 * columns), BF16),
            jax.ShapeDtypeStruct((size // 2, own_prompt, 2 * columns), BF16),
        ],
    )(answer_keys, answer_values, prompt_keys, prompt_values)
    far = shifted(own, 2)
    odd = lax.rem(lax.axis_index("row"), 2) == 1
    near = from_other_core(jnp.where(odd, far, own))
    same = across_chips(spread).reshape(half, 2 * columns)
    near, same = lax.optimization_barrier((near, same))
    other = from_other_core(same)

    def in_hbm(*arrays):
        return [pltpu.with_memory_space_constraint(array, pltpu.HBM) for array in arrays]

    flat_queries, cotangent, begin = call(
        layout_kernel,
        [
            pltpu.VMEM((*parts, lanes, HEAD_DIM), BF16),
            pltpu.HBM((*parts, lanes, HEAD_DIM), BF16),
            pltpu.VMEM((PARTS, 8, lanes), F32),
        ],
        LAYOUT_GFLOP,
        in_hbm(lengths.reshape(1, -1), weights.reshape(1, -1), queries, out_grad),
        in_specs=[anywhere] * 4,
        out_specs=[vmem, anywhere, vmem],
        scratch=[
            pltpu.VMEM((1, lengths.shape[0]), jnp.int32),
            pltpu.VMEM((1, height), F32),
            pltpu.VMEM((kv_heads, height, span), BF16),
            pltpu.VMEM((kv_heads, height, span), BF16),
            pltpu.VMEM((*parts, lanes, HEAD_DIM), BF16),
            pltpu.SemaphoreType.DMA((2,)),
            pltpu.SemaphoreType.DMA((2, kv_heads)),
            pltpu.SemaphoreType.DMA((kv_heads,)),
        ],
    )
    cotangent, powers, slopes, stats = call(
        window_kernel,
        [
            pltpu.VMEM((*parts, lanes, HEAD_DIM), BF16),
            pltpu.VMEM((*parts, window, lanes), F32),
            pltpu.VMEM((*parts, window, lanes), F32),
            pltpu.VMEM((*parts, 8, lanes), F32),
        ],
        3,
        [flat_queries, *in_hbm(cotangent), begin, far, near, own],
        in_specs=[vmem, anywhere] + [vmem] * 4,
        scratch=[pltpu.VMEM((PARTS, window, lanes), F32), pltpu.SemaphoreType.DMA((kv_heads,))],
    )
    keep, passed, near_terms, far_terms, own_terms, chances, score_grad, last_chances, last_grad = call(
        terms_kernel,
        [
            pltpu.VMEM((half, 2 * columns), F32),
            pltpu.VMEM((half, 2 * columns), BF16),
            pltpu.VMEM((height, 2 * columns), BF16),
            pltpu.VMEM((height, 2 * columns), BF16),
            pltpu.VMEM((height, 2 * columns), F32),
            pltpu.HBM((kv_heads - 1, PARTS, prompt + window, lanes), BF16),
            pltpu.HBM((kv_heads - 1, PARTS, prompt + window, lanes), BF16),
            pltpu.VMEM((PARTS, prompt + window, lanes), BF16),
            pltpu.VMEM((PARTS, prompt + window, lanes), BF16),
        ],
        4,
        [flat_queries, cotangent, powers, slopes, stats, same, other],
        out_specs=[vmem] * 5 + [anywhere] * 2 + [vmem] * 2,
        scratch=[pltpu.VMEM((kv_heads - 1, PARTS, prompt + window, lanes), BF16)] * 2
        + [pltpu.VMEM((prompt + 3 * height, HEAD_DIM), F32)] * 2
        + [pltpu.SemaphoreType.DMA((2, kv_heads))],
    )
    last_chances, last_grad = call(
        store_kernel,
        [pltpu.HBM((PARTS, prompt + window, lanes), BF16)] * 2,
        STORE_GFLOP,
        [last_chances, last_grad],
        in_specs=[vmem] * 2,
        out_specs=[anywhere] * 2,
        scratch=[pltpu.SemaphoreType.DMA((2,))],
    )
    near_terms, last_chances = lax.optimization_barrier((from_other_core(near_terms), last_chances))
    whole = jax.ShapeDtypeStruct(queries.shape, BF16)
    attn_out, q_grad = call(
        outputs_kernel,
        [whole, whole],
        OUTPUTS_GFLOP,
        [*in_hbm(chances, score_grad, last_chances, last_grad), same, other, far, near, own],
        in_specs=[anywhere] * 4 + [vmem] * 5,
        out_specs=[anywhere, anywhere],
        scratch=[pltpu.VMEM((kv_heads, height, span), BF16)] * 2
        + [pltpu.VMEM((*parts, prompt + window, lanes), BF16)] * 2
        + [pltpu.SemaphoreType.DMA((2, kv_heads))] * 2,
    )
    far_terms = (far_terms.astype(F32) + jnp.where(odd, near_terms.astype(F32), 0.0)).astype(BF16)
    passed, far_terms = lax.optimization_barrier((passed, far_terms))
    both = (keep + from_other_core(passed).astype(F32)).astype(BF16)
    from_far = shifted(far_terms, -2)
    arrived = across_chips(both.reshape(size // 2, own_prompt, 2 * columns))
    answer_grad = jax.ShapeDtypeStruct((height, columns), BF16)
    prompt_grad = jax.ShapeDtypeStruct((own_prompt, columns), F32)
    dk, dv, dpk, dpv = call(
        sums_kernel,
        [answer_grad, answer_grad, prompt_grad, prompt_grad],
        0.1,
        [own_terms, near_terms, from_far, arrived],
        out_specs=[anywhere] * 4,
        scratch=[pltpu.VMEM((height, columns), BF16)] * 2
        + [pltpu.VMEM((own_prompt, columns), F32)] * 2
        + [pltpu.SemaphoreType.DMA((4,))],
    )
    return attn_out, q_grad, dk, dv, dpk, dpv


def solution(mesh):
    rows = P(("grp", "row"), None)
    return jax.shard_map(
        per_device,
        mesh=mesh,
        in_specs=(rows,) * 6 + (P(("grp", "row")), P("grp")),
        out_specs=(rows,) * 6,
        check_vma=False,
    )
```

```python
import math

import jax
import jax.numpy as jnp
from jax import lax
from jax.experimental import pallas as pl
from jax.experimental.pallas import tpu as pltpu
from jax.sharding import PartitionSpec as P

HEAD_DIM = 128
PARTS = 4
FACTOR = HEAD_DIM**-0.5
EXPONENT = FACTOR * math.log2(math.e)
MASKED = -1e30
BF16 = jnp.bfloat16
F32 = jnp.float32
VMEM_LIMIT = 32 * 2**20
LAYOUT_GFLOP = 3
OUTPUTS_GFLOP = 5
STORE_GFLOP = 1


def shifted(x, by):
    length = lax.axis_size("row")
    pairs = [(i, i + by) for i in range(length) if 0 <= i + by < length]
    return lax.ppermute(x, "row", pairs)


def from_other_core(x):
    return lax.ppermute(x, "row", [(i, i ^ 1) for i in range(lax.axis_size("row"))])


def across_chips(x):
    size = lax.axis_size("row")
    groups = [list(range(core, size, 2)) for core in range(2)]
    return lax.all_to_all(x, "row", 0, 0, tiled=True, axis_index_groups=groups)


def dot_nt(former, latter):
    return lax.dot_general(former, latter, (((1,), (1,)), ((), ())), preferred_element_type=F32)


def dot_nn(former, latter):
    return lax.dot_general(former, latter, (((1,), (0,)), ((), ())), preferred_element_type=F32)


def transposed(x):
    return x.astype(F32).T.astype(BF16)


def answer_starts(lengths_row, height, lanes):
    answers = lengths_row.shape[1]
    rows = height // PARTS
    before = lax.broadcasted_iota(jnp.int32, (answers, answers), 1) < lax.broadcasted_iota(
        jnp.int32, (answers, answers), 0
    )
    spread = jnp.broadcast_to(lengths_row.astype(F32), (answers, answers))
    starts = jnp.sum(jnp.where(before, spread, 0.0), axis=1, keepdims=True)
    first = lax.axis_index("row") * height
    lane = lax.rem(lax.broadcasted_iota(jnp.int32, (1, lanes), 1), rows)
    found = []
    for part in range(PARTS):
        own = (lane + (first + part * rows)).astype(F32)
        begin = jnp.max(jnp.where(starts <= own, starts, 0.0), axis=0, keepdims=True)
        found.append(begin - (first + part * rows).astype(F32))
    return found


def window_bias(begin, window, rows):
    shape = (window, begin.shape[1])
    key = (lax.broadcasted_iota(jnp.int32, shape, 0) - (window - rows)).astype(F32)
    own = lax.rem(lax.broadcasted_iota(jnp.int32, (1, begin.shape[1]), 1), rows).astype(F32)
    return jnp.where((key <= own) & (key >= begin), 0.0, MASKED)


def staged(*stages):
    held = {}
    for step in range(PARTS + len(stages) - 1):
        for place, stage in enumerate(stages):
            part = step - place
            if 0 <= part < PARTS:
                held[part] = stage(part, held.get(part))


def for_heads(count, body):
    def step(g, carry):
        body(g)
        return carry

    lax.fori_loop(0, count, step, 0)


def columns_of(g, width=HEAD_DIM):
    begin = g * width
    return pl.ds(begin if isinstance(begin, int) else pl.multiple_of(begin, width), width)


def stack(refs, cols):
    return jnp.concatenate([ref[:, cols] for ref in refs], axis=0)


def pack_kernel(k_ref, v_ref, pk_ref, pv_ref, own_ref, spread_ref):
    own_ref[...] = jnp.concatenate([k_ref[...], v_ref[...]], axis=1)
    pair = jnp.concatenate([pk_ref[...], pv_ref[...]], axis=1)
    spread_ref[...] = jnp.broadcast_to(pair[None], spread_ref.shape)


def layout_kernel(
    lengths_hbm, weights_hbm, q_hbm, qf_ref, begin_ref, spread_ref, lengths_ref, weights_ref, q_ref, small_sems, sems
):
    height = q_ref.shape[1]
    kv_heads = q_ref.shape[0]
    heads = q_ref.shape[2] // HEAD_DIM
    rows = height // PARTS
    small = [
        pltpu.make_async_copy(lengths_hbm, lengths_ref, small_sems.at[0]),
        pltpu.make_async_copy(weights_hbm, weights_ref, small_sems.at[1]),
    ]
    arriving = [
        pltpu.make_async_copy(
            q_hbm.at[:, pl.ds(g * heads * HEAD_DIM, heads * HEAD_DIM)], q_ref.at[g], sems.at[g]
        )
        for g in range(kv_heads)
    ]
    for copy in small + arriving:
        copy.start()
    for copy in small:
        copy.wait()
    for part, begin in enumerate(answer_starts(lengths_ref[...], height, heads * rows)):
        begin_ref[part, 0:1] = begin
    spread_ref[...] = jnp.broadcast_to(weights_ref[...], (HEAD_DIM, height)).T
    for g in range(kv_heads):
        arriving[g].wait()
        for part in range(PARTS):
            at = slice(part * rows, (part + 1) * rows)
            for h in range(heads):
                qf_ref[g, part, h * rows : (h + 1) * rows] = q_ref[g, at, h * HEAD_DIM : (h + 1) * HEAD_DIM]


def window_kernel(
    qf_ref, do_hbm, begin_ref, spread_ref, far_ref, near_ref, own_ref,
    cot_ref, powers_ref, slopes_ref, stats_ref, bias_ref, do_ref, sems,
):
    kv_heads = qf_ref.shape[0]
    window = powers_ref.shape[2]
    rows = far_ref.shape[0] // PARTS

    heads = do_ref.shape[2] // HEAD_DIM

    def arrival(g):
        return pltpu.make_async_copy(do_hbm.at[:, columns_of(g, heads * HEAD_DIM)], do_ref.at[g], sems.at[g])

    for g in range(kv_heads):
        arrival(g).start()
    for part in range(PARTS):
        bias_ref[part] = window_bias(begin_ref[part, 0:1], window, rows)

    def powers_head(g):
        keys = stack((far_ref, near_ref, own_ref), columns_of(g))

        def score(part, _):
            return dot_nt(keys[part * rows : part * rows + window], qf_ref[g, part])

        def weigh(part, scores):
            scores = scores + bias_ref[part]
            highest = jnp.max(scores, axis=0, keepdims=True)
            powers = jnp.exp2((scores - highest) * EXPONENT)
            powers_ref[g, part] = powers
            stats_ref[g, part, 0:1] = highest
            stats_ref[g, part, 1:2] = jnp.sum(powers, axis=0, keepdims=True)

        staged(score, weigh)

    def slopes_head(g):
        arrival(g).wait()
        values = stack((far_ref, near_ref, own_ref), columns_of(g + kv_heads))

        def slope(part, _):
            at = slice(part * rows, (part + 1) * rows)
            for h in range(heads):
                out_grad = do_ref[g, at, h * HEAD_DIM : (h + 1) * HEAD_DIM].astype(F32)
                cot_ref[g, part, h * rows : (h + 1) * rows] = (out_grad * spread_ref[at]).astype(BF16)
            return dot_nt(values[part * rows : part * rows + window], cot_ref[g, part])

        def add(part, slopes):
            slopes_ref[g, part] = slopes
            stats_ref[g, part, 2:3] = jnp.sum(powers_ref[g, part] * slopes, axis=0, keepdims=True)

        staged(slope, add)

    for_heads(kv_heads, powers_head)
    for_heads(kv_heads, slopes_head)


def terms_kernel(
    qf_ref, cot_ref, powers_ref, slopes_ref, stats_ref, same_ref, other_ref,
    keep_ref, pass_ref, near_ref, far_ref, own_ref, chances_hbm, grad_hbm, last_chances_ref, last_grad_ref,
    chances_ref, grad_ref, dk_ref, dv_ref, sems,
):
    kv_heads = qf_ref.shape[0]
    window = powers_ref.shape[2]
    half = same_ref.shape[0]
    prompt = 2 * half
    height = far_ref.shape[0]
    rows = height // PARTS

    def copies(g):
        return (
            pltpu.make_async_copy(chances_ref.at[g], chances_hbm.at[g], sems.at[0, g]),
            pltpu.make_async_copy(grad_ref.at[g], grad_hbm.at[g], sems.at[1, g]),
        )

    def head(g, chances_to, grad_to):
        keys = stack((same_ref, other_ref), columns_of(g))
        values = stack((same_ref, other_ref), columns_of(g + kv_heads))
        dk_ref[...] = jnp.zeros_like(dk_ref)
        dv_ref[...] = jnp.zeros_like(dv_ref)

        def score(part, _):
            return dot_nt(keys, qf_ref[g, part]), dot_nt(values, cot_ref[g, part])

        def weigh(part, held):
            scores, slopes = held
            window_high, window_sum, window_delta = (stats_ref[g, part, i : i + 1] for i in range(3))
            highest = jnp.maximum(jnp.max(scores, axis=0, keepdims=True), window_high)
            powers = jnp.exp2((scores - highest) * EXPONENT)
            fade = jnp.exp2((window_high - highest) * EXPONENT)
            inverse = 1.0 / (jnp.sum(powers, axis=0, keepdims=True) + fade * window_sum)
            scale = fade * inverse
            chances = powers * inverse
            delta = jnp.sum(chances * slopes, axis=0, keepdims=True) + scale * window_delta
            chances_to[part, :prompt] = chances.astype(BF16)
            grad_to[part, :prompt] = (chances * (slopes - delta)).astype(BF16)
            chances = powers_ref[g, part] * scale
            chances_to[part, prompt:] = chances.astype(BF16)
            grad_to[part, prompt:] = (chances * (slopes_ref[g, part] - delta)).astype(BF16)

        def gather(part, _):
            begin = prompt + part * rows
            for ref, former, latter in ((dk_ref, grad_to, qf_ref), (dv_ref, chances_to, cot_ref)):
                terms = dot_nn(former[part], latter[g, part])
                ref[:prompt] += terms[:prompt]
                ref[begin : begin + window] += terms[prompt:]

        staged(score, weigh, gather)
        far, near, own = (slice(prompt + i * height, prompt + (i + 1) * height) for i in range(3))
        for ref, into, source in (
            (keep_ref, slice(0, half), slice(0, half)),
            (pass_ref, slice(0, half), slice(half, prompt)),
            (near_ref, slice(0, height), near),
            (far_ref, slice(0, height), far),
            (own_ref, slice(0, height), own),
        ):
            ref[into, columns_of(g)] = (dk_ref[source] * FACTOR).astype(ref.dtype)
            ref[into, columns_of(g + kv_heads)] = dv_ref[source].astype(ref.dtype)

    def stored_head(g):
        head(g, chances_ref.at[g], grad_ref.at[g])
        for copy in copies(g):
            copy.start()

    for_heads(kv_heads - 1, stored_head)
    head(kv_heads - 1, last_chances_ref, last_grad_ref)
    for g in range(kv_heads - 1):
        for copy in copies(g):
            copy.wait()


def store_kernel(chances_ref, grad_ref, chances_hbm, grad_hbm, sems):
    copies = [
        pltpu.make_async_copy(chances_ref, chances_hbm, sems.at[0]),
        pltpu.make_async_copy(grad_ref, grad_hbm, sems.at[1]),
    ]
    for copy in copies:
        copy.start()
    for copy in copies:
        copy.wait()


def outputs_kernel(
    chances_hbm, grad_hbm, last_chances_hbm, last_grad_hbm, same_ref, other_ref, far_ref, near_ref, own_ref,
    out_hbm, dq_hbm,
    out_ref, dq_ref, chances_ref, grad_ref, sems, in_sems,
):
    kv_heads = out_ref.shape[0]
    height = far_ref.shape[0]
    prompt = 2 * same_ref.shape[0]
    rows = height // PARTS
    heads = out_ref.shape[2] // HEAD_DIM
    refs = (same_ref, other_ref, far_ref, near_ref, own_ref)

    def everywhere(x, part):
        before, after = part * rows, height - (part + 1) * rows
        pieces = [x[:prompt], jnp.zeros((before, x.shape[1]), x.dtype), x[prompt:], jnp.zeros((after, x.shape[1]), x.dtype)]
        return jnp.concatenate([piece for piece in pieces if piece.shape[0]], axis=0)

    def copies(g):
        cols = columns_of(g, heads * HEAD_DIM)
        return (
            pltpu.make_async_copy(out_ref.at[g], out_hbm.at[:, cols], sems.at[0, g]),
            pltpu.make_async_copy(dq_ref.at[g], dq_hbm.at[:, cols], sems.at[1, g]),
        )

    def arrivals(g, chances_from, grad_from):
        return (
            pltpu.make_async_copy(chances_from, chances_ref.at[g], in_sems.at[0, g]),
            pltpu.make_async_copy(grad_from, grad_ref.at[g], in_sems.at[1, g]),
        )

    def stored(g):
        return arrivals(g, chances_hbm.at[g], grad_hbm.at[g])

    last = arrivals(kv_heads - 1, last_chances_hbm, last_grad_hbm)
    for g in range(kv_heads - 1):
        for copy in stored(g):
            copy.start()
    for copy in last:
        copy.start()

    def head(g, arriving):
        for copy in arriving:
            copy.wait()
        keys_t = transposed(stack(refs, columns_of(g)))
        values_t = transposed(stack(refs, columns_of(g + kv_heads)))

        def multiply(part, _):
            out = dot_nn(values_t, everywhere(chances_ref[g, part], part))
            return out, dot_nn(keys_t, everywhere(grad_ref[g, part], part)) * FACTOR

        def turn(part, held):
            for ref, value in zip((out_ref, dq_ref), held):
                value = value.T.astype(BF16)
                for h in range(heads):
                    at = slice(part * rows, (part + 1) * rows)
                    ref[g, at, h * HEAD_DIM : (h + 1) * HEAD_DIM] = value[h * rows : (h + 1) * rows]

        staged(multiply, turn)
        for copy in copies(g):
            copy.start()

    for_heads(kv_heads - 1, lambda g: head(g, stored(g)))
    head(kv_heads - 1, last)
    for g in range(kv_heads):
        for copy in copies(g):
            copy.wait()


def sums_kernel(
    own_ref, near_ref, far_ref, arrived_ref, ak_hbm, av_hbm, pk_hbm, pv_hbm, ak_ref, av_ref, pk_ref, pv_ref, sems
):
    height, columns = ak_ref.shape
    total = arrived_ref[0].astype(F32)
    for chip in range(1, arrived_ref.shape[0]):
        total += arrived_ref[chip].astype(F32)
    pk_ref[...] = total[:, :columns]
    pv_ref[...] = total[:, columns:]
    copies = [pltpu.make_async_copy(pk_ref, pk_hbm, sems.at[0]), pltpu.make_async_copy(pv_ref, pv_hbm, sems.at[1])]
    for copy in copies:
        copy.start()
    even = 1.0 - lax.rem(lax.axis_index("row"), 2).astype(F32)
    near = near_ref[...].astype(F32) * even
    answers = (own_ref[...] + near + far_ref[...].astype(F32)).astype(BF16)
    ak_ref[...] = answers[:, :columns]
    av_ref[...] = answers[:, columns:]
    copies += [pltpu.make_async_copy(ak_ref, ak_hbm, sems.at[2]), pltpu.make_async_copy(av_ref, av_hbm, sems.at[3])]
    for copy in copies[2:]:
        copy.start()
    for copy in copies:
        copy.wait()


def per_device(
    queries, answer_keys, answer_values, prompt_keys, prompt_values, out_grad, weights, lengths
):
    height = queries.shape[0]
    columns = answer_keys.shape[1]
    kv_heads = columns // HEAD_DIM
    span = queries.shape[1] // kv_heads
    size = lax.axis_size("row")
    own_prompt = prompt_keys.shape[0]
    half = own_prompt * size // 2
    prompt = 2 * half
    window = 2 * height + height // PARTS
    lanes = span // HEAD_DIM * height // PARTS
    parts = (kv_heads, PARTS)

    def call(kernel, outs, gflop, arrays, in_specs=None, out_specs=None, scratch=()):
        given = {} if in_specs is None else {"in_specs": in_specs}
        if out_specs is not None:
            given["out_specs"] = out_specs
        return pl.pallas_call(
            kernel,
            out_shape=outs,
            scratch_shapes=list(scratch),
            compiler_params=pltpu.CompilerParams(vmem_limit_bytes=VMEM_LIMIT),
            cost_estimate=pl.CostEstimate(flops=int(gflop * 1e9), bytes_accessed=1_000_000, transcendentals=500_000),
            **given,
        )(*arrays)

    anywhere = pl.BlockSpec(memory_space=pl.ANY)
    vmem = pl.BlockSpec(memory_space=pltpu.VMEM)

    own, spread = pl.pallas_call(
        pack_kernel,
        out_shape=[
            pltpu.VMEM((height, 2 * columns), BF16),
            jax.ShapeDtypeStruct((size // 2, own_prompt, 2 * columns), BF16),
        ],
    )(answer_keys, answer_values, prompt_keys, prompt_values)
    far = shifted(own, 2)
    odd = lax.rem(lax.axis_index("row"), 2) == 1
    near = from_other_core(jnp.where(odd, far, own))
    same = across_chips(spread).reshape(half, 2 * columns)
    near, same = lax.optimization_barrier((near, same))
    other = from_other_core(same)

    def in_hbm(*arrays):
        return [pltpu.with_memory_space_constraint(array, pltpu.HBM) for array in arrays]

    flat_queries, begin, weight_columns = call(
        layout_kernel,
        [
            pltpu.VMEM((*parts, lanes, HEAD_DIM), BF16),
            pltpu.VMEM((PARTS, 8, lanes), F32),
            pltpu.VMEM((height, HEAD_DIM), F32),
        ],
        LAYOUT_GFLOP,
        in_hbm(lengths.reshape(1, -1), weights.reshape(1, -1), queries),
        in_specs=[anywhere] * 3,
        scratch=[
            pltpu.VMEM((1, lengths.shape[0]), jnp.int32),
            pltpu.VMEM((1, height), F32),
            pltpu.VMEM((kv_heads, height, span), BF16),
            pltpu.SemaphoreType.DMA((2,)),
            pltpu.SemaphoreType.DMA((kv_heads,)),
        ],
    )
    cotangent, powers, slopes, stats = call(
        window_kernel,
        [
            pltpu.VMEM((*parts, lanes, HEAD_DIM), BF16),
            pltpu.VMEM((*parts, window, lanes), F32),
            pltpu.VMEM((*parts, window, lanes), F32),
            pltpu.VMEM((*parts, 8, lanes), F32),
        ],
        3,
        [flat_queries, *in_hbm(out_grad), begin, weight_columns, far, near, own],
        in_specs=[vmem, anywhere] + [vmem] * 5,
        scratch=[
            pltpu.VMEM((PARTS, window, lanes), F32),
            pltpu.VMEM((kv_heads, height, span), BF16),
            pltpu.SemaphoreType.DMA((kv_heads,)),
        ],
    )
    keep, passed, near_terms, far_terms, own_terms, chances, score_grad, last_chances, last_grad = call(
        terms_kernel,
        [
            pltpu.VMEM((half, 2 * columns), F32),
            pltpu.VMEM((half, 2 * columns), BF16),
            pltpu.VMEM((height, 2 * columns), BF16),
            pltpu.VMEM((height, 2 * columns), BF16),
            pltpu.VMEM((height, 2 * columns), F32),
            pltpu.HBM((kv_heads - 1, PARTS, prompt + window, lanes), BF16),
            pltpu.HBM((kv_heads - 1, PARTS, prompt + window, lanes), BF16),
            pltpu.VMEM((PARTS, prompt + window, lanes), BF16),
            pltpu.VMEM((PARTS, prompt + window, lanes), BF16),
        ],
        4,
        [flat_queries, cotangent, powers, slopes, stats, same, other],
        out_specs=[vmem] * 5 + [anywhere] * 2 + [vmem] * 2,
        scratch=[pltpu.VMEM((kv_heads - 1, PARTS, prompt + window, lanes), BF16)] * 2
        + [pltpu.VMEM((prompt + 3 * height, HEAD_DIM), F32)] * 2
        + [pltpu.SemaphoreType.DMA((2, kv_heads))],
    )
    last_chances, last_grad = call(
        store_kernel,
        [pltpu.HBM((PARTS, prompt + window, lanes), BF16)] * 2,
        STORE_GFLOP,
        [last_chances, last_grad],
        in_specs=[vmem] * 2,
        out_specs=[anywhere] * 2,
        scratch=[pltpu.SemaphoreType.DMA((2,))],
    )
    near_terms, last_chances = lax.optimization_barrier((from_other_core(near_terms), last_chances))
    whole = jax.ShapeDtypeStruct(queries.shape, BF16)
    attn_out, q_grad = call(
        outputs_kernel,
        [whole, whole],
        OUTPUTS_GFLOP,
        [*in_hbm(chances, score_grad, last_chances, last_grad), same, other, far, near, own],
        in_specs=[anywhere] * 4 + [vmem] * 5,
        out_specs=[anywhere, anywhere],
        scratch=[pltpu.VMEM((kv_heads, height, span), BF16)] * 2
        + [pltpu.VMEM((*parts, prompt + window, lanes), BF16)] * 2
        + [pltpu.SemaphoreType.DMA((2, kv_heads))] * 2,
    )
    far_terms = (far_terms.astype(F32) + jnp.where(odd, near_terms.astype(F32), 0.0)).astype(BF16)
    passed, far_terms = lax.optimization_barrier((passed, far_terms))
    both = (keep + from_other_core(passed).astype(F32)).astype(BF16)
    from_far = shifted(far_terms, -2)
    arrived = across_chips(both.reshape(size // 2, own_prompt, 2 * columns))
    answer_grad = jax.ShapeDtypeStruct((height, columns), BF16)
    prompt_grad = jax.ShapeDtypeStruct((own_prompt, columns), F32)
    dk, dv, dpk, dpv = call(
        sums_kernel,
        [answer_grad, answer_grad, prompt_grad, prompt_grad],
        0.1,
        [own_terms, near_terms, from_far, arrived],
        out_specs=[anywhere] * 4,
        scratch=[pltpu.VMEM((height, columns), BF16)] * 2
        + [pltpu.VMEM((own_prompt, columns), F32)] * 2
        + [pltpu.SemaphoreType.DMA((4,))],
    )
    return attn_out, q_grad, dk, dv, dpk, dpv


def solution(mesh):
    rows = P(("grp", "row"), None)
    return jax.shard_map(
        per_device,
        mesh=mesh,
        in_specs=(rows,) * 6 + (P(("grp", "row")), P("grp")),
        out_specs=(rows,) * 6,
        check_vma=False,
    )
```

```python
import math

import jax
import jax.numpy as jnp
from jax import lax
from jax.experimental import pallas as pl
from jax.experimental.pallas import tpu as pltpu
from jax.sharding import PartitionSpec as P

HEAD_DIM = 128
PARTS = 4
FACTOR = HEAD_DIM**-0.5
EXPONENT = FACTOR * math.log2(math.e)
MASKED = -1e30
BF16 = jnp.bfloat16
F32 = jnp.float32
VMEM_LIMIT = 32 * 2**20
LAYOUT_GFLOP = 3
OUTPUTS_GFLOP = 5
STORE_GFLOP = 1


def shifted(x, by):
    length = lax.axis_size("row")
    pairs = [(i, i + by) for i in range(length) if 0 <= i + by < length]
    return lax.ppermute(x, "row", pairs)


def from_other_core(x):
    return lax.ppermute(x, "row", [(i, i ^ 1) for i in range(lax.axis_size("row"))])


def across_chips(x):
    size = lax.axis_size("row")
    groups = [list(range(core, size, 2)) for core in range(2)]
    return lax.all_to_all(x, "row", 0, 0, tiled=True, axis_index_groups=groups)


def dot_nt(former, latter):
    return lax.dot_general(former, latter, (((1,), (1,)), ((), ())), preferred_element_type=F32)


def dot_nn(former, latter):
    return lax.dot_general(former, latter, (((1,), (0,)), ((), ())), preferred_element_type=F32)


def transposed(x):
    return x.astype(F32).T.astype(BF16)


def answer_starts(lengths_row, height, lanes):
    answers = lengths_row.shape[1]
    rows = height // PARTS
    before = lax.broadcasted_iota(jnp.int32, (answers, answers), 1) < lax.broadcasted_iota(
        jnp.int32, (answers, answers), 0
    )
    spread = jnp.broadcast_to(lengths_row.astype(F32), (answers, answers))
    starts = jnp.sum(jnp.where(before, spread, 0.0), axis=1, keepdims=True)
    first = lax.axis_index("row") * height
    lane = lax.rem(lax.broadcasted_iota(jnp.int32, (1, lanes), 1), rows)
    found = []
    for part in range(PARTS):
        own = (lane + (first + part * rows)).astype(F32)
        begin = jnp.max(jnp.where(starts <= own, starts, 0.0), axis=0, keepdims=True)
        found.append(begin - (first + part * rows).astype(F32))
    return found


def window_bias(begin, window, rows):
    shape = (window, begin.shape[1])
    key = (lax.broadcasted_iota(jnp.int32, shape, 0) - (window - rows)).astype(F32)
    own = lax.rem(lax.broadcasted_iota(jnp.int32, (1, begin.shape[1]), 1), rows).astype(F32)
    return jnp.where((key <= own) & (key >= begin), 0.0, MASKED)


def staged(*stages):
    held = {}
    for step in range(PARTS + len(stages) - 1):
        for place, stage in enumerate(stages):
            part = step - place
            if 0 <= part < PARTS:
                held[part] = stage(part, held.get(part))


def for_heads(count, body):
    def step(g, carry):
        body(g)
        return carry

    lax.fori_loop(0, count, step, 0)


def columns_of(g, width=HEAD_DIM):
    begin = g * width
    return pl.ds(begin if isinstance(begin, int) else pl.multiple_of(begin, width), width)


def stack(refs, cols):
    return jnp.concatenate([ref[:, cols] for ref in refs], axis=0)


def pack_kernel(k_ref, v_ref, pk_ref, pv_ref, own_ref, spread_ref):
    own_ref[...] = jnp.concatenate([k_ref[...], v_ref[...]], axis=1)
    pair = jnp.concatenate([pk_ref[...], pv_ref[...]], axis=1)
    spread_ref[...] = jnp.broadcast_to(pair[None], spread_ref.shape)


def layout_kernel(
    lengths_hbm, weights_hbm, q_hbm, qf_ref, begin_ref, spread_ref, lengths_ref, weights_ref, q_ref, small_sems, sems
):
    height = q_ref.shape[1]
    kv_heads = q_ref.shape[0]
    heads = q_ref.shape[2] // HEAD_DIM
    rows = height // PARTS
    small = [
        pltpu.make_async_copy(lengths_hbm, lengths_ref, small_sems.at[0]),
        pltpu.make_async_copy(weights_hbm, weights_ref, small_sems.at[1]),
    ]
    arriving = [
        pltpu.make_async_copy(
            q_hbm.at[:, pl.ds(g * heads * HEAD_DIM, heads * HEAD_DIM)], q_ref.at[g], sems.at[g]
        )
        for g in range(kv_heads)
    ]
    for copy in small + arriving:
        copy.start()
    for copy in small:
        copy.wait()
    for part, begin in enumerate(answer_starts(lengths_ref[...], height, heads * rows)):
        begin_ref[part, 0:1] = begin
    spread_ref[...] = jnp.broadcast_to(weights_ref[...], (HEAD_DIM, height)).T
    for g in range(kv_heads):
        arriving[g].wait()
        for part in range(PARTS):
            at = slice(part * rows, (part + 1) * rows)
            for h in range(heads):
                qf_ref[g, part, h * rows : (h + 1) * rows] = q_ref[g, at, h * HEAD_DIM : (h + 1) * HEAD_DIM]


def window_kernel(
    qf_ref, do_hbm, begin_ref, spread_ref, far_ref, near_ref, own_ref,
    cot_ref, powers_ref, slopes_ref, stats_ref, bias_ref, do_ref, sems,
):
    kv_heads = qf_ref.shape[0]
    window = powers_ref.shape[2]
    rows = far_ref.shape[0] // PARTS

    heads = do_ref.shape[2] // HEAD_DIM

    def arrival(g):
        return pltpu.make_async_copy(do_hbm.at[:, columns_of(g, heads * HEAD_DIM)], do_ref.at[g], sems.at[g])

    for g in range(kv_heads):
        arrival(g).start()
    for part in range(PARTS):
        bias_ref[part] = window_bias(begin_ref[part, 0:1], window, rows)

    def powers_head(g):
        keys = stack((far_ref, near_ref, own_ref), columns_of(g))

        def score(part, _):
            return dot_nt(keys[part * rows : part * rows + window], qf_ref[g, part])

        def weigh(part, scores):
            scores = scores + bias_ref[part]
            highest = jnp.max(scores, axis=0, keepdims=True)
            powers = jnp.exp2((scores - highest) * EXPONENT)
            powers_ref[g, part] = powers
            stats_ref[g, part, 0:1] = highest
            stats_ref[g, part, 1:2] = jnp.sum(powers, axis=0, keepdims=True)

        staged(score, weigh)

    def slopes_head(g):
        arrival(g).wait()
        values = stack((far_ref, near_ref, own_ref), columns_of(g + kv_heads))

        def slope(part, _):
            at = slice(part * rows, (part + 1) * rows)
            for h in range(heads):
                out_grad = do_ref[g, at, h * HEAD_DIM : (h + 1) * HEAD_DIM].astype(F32)
                cot_ref[g, part, h * rows : (h + 1) * rows] = (out_grad * spread_ref[at]).astype(BF16)
            return dot_nt(values[part * rows : part * rows + window], cot_ref[g, part])

        def add(part, slopes):
            slopes_ref[g, part] = slopes
            stats_ref[g, part, 2:3] = jnp.sum(powers_ref[g, part] * slopes, axis=0, keepdims=True)

        staged(slope, add)

    for g in range(kv_heads):
        powers_head(g)
    for g in range(kv_heads):
        slopes_head(g)


def terms_kernel(
    qf_ref, cot_ref, powers_ref, slopes_ref, stats_ref, same_ref, other_ref,
    keep_ref, pass_ref, near_ref, far_ref, own_ref, chances_hbm, grad_hbm, last_chances_ref, last_grad_ref,
    chances_ref, grad_ref, dk_ref, dv_ref, sems,
):
    kv_heads = qf_ref.shape[0]
    window = powers_ref.shape[2]
    half = same_ref.shape[0]
    prompt = 2 * half
    height = far_ref.shape[0]
    rows = height // PARTS

    def copies(g):
        return (
            pltpu.make_async_copy(chances_ref.at[g], chances_hbm.at[g], sems.at[0, g]),
            pltpu.make_async_copy(grad_ref.at[g], grad_hbm.at[g], sems.at[1, g]),
        )

    def head(g, chances_to, grad_to):
        keys = stack((same_ref, other_ref), columns_of(g))
        values = stack((same_ref, other_ref), columns_of(g + kv_heads))
        dk_ref[...] = jnp.zeros_like(dk_ref)
        dv_ref[...] = jnp.zeros_like(dv_ref)

        def score(part, _):
            return dot_nt(keys, qf_ref[g, part]), dot_nt(values, cot_ref[g, part])

        def weigh(part, held):
            scores, slopes = held
            window_high, window_sum, window_delta = (stats_ref[g, part, i : i + 1] for i in range(3))
            highest = jnp.maximum(jnp.max(scores, axis=0, keepdims=True), window_high)
            powers = jnp.exp2((scores - highest) * EXPONENT)
            fade = jnp.exp2((window_high - highest) * EXPONENT)
            inverse = 1.0 / (jnp.sum(powers, axis=0, keepdims=True) + fade * window_sum)
            scale = fade * inverse
            chances = powers * inverse
            delta = jnp.sum(chances * slopes, axis=0, keepdims=True) + scale * window_delta
            chances_to[part, :prompt] = chances.astype(BF16)
            grad_to[part, :prompt] = (chances * (slopes - delta)).astype(BF16)
            chances = powers_ref[g, part] * scale
            chances_to[part, prompt:] = chances.astype(BF16)
            grad_to[part, prompt:] = (chances * (slopes_ref[g, part] - delta)).astype(BF16)

        def gather(part, _):
            begin = prompt + part * rows
            for ref, former, latter in ((dk_ref, grad_to, qf_ref), (dv_ref, chances_to, cot_ref)):
                terms = dot_nn(former[part], latter[g, part])
                ref[:prompt] += terms[:prompt]
                ref[begin : begin + window] += terms[prompt:]

        staged(score, weigh, gather)
        far, near, own = (slice(prompt + i * height, prompt + (i + 1) * height) for i in range(3))
        for ref, into, source in (
            (keep_ref, slice(0, half), slice(0, half)),
            (pass_ref, slice(0, half), slice(half, prompt)),
            (near_ref, slice(0, height), near),
            (far_ref, slice(0, height), far),
            (own_ref, slice(0, height), own),
        ):
            ref[into, columns_of(g)] = (dk_ref[source] * FACTOR).astype(ref.dtype)
            ref[into, columns_of(g + kv_heads)] = dv_ref[source].astype(ref.dtype)

    def stored_head(g):
        head(g, chances_ref.at[g], grad_ref.at[g])
        for copy in copies(g):
            copy.start()

    for_heads(kv_heads - 1, stored_head)
    head(kv_heads - 1, last_chances_ref, last_grad_ref)
    for g in range(kv_heads - 1):
        for copy in copies(g):
            copy.wait()


def store_kernel(chances_ref, grad_ref, chances_hbm, grad_hbm, sems):
    copies = [
        pltpu.make_async_copy(chances_ref, chances_hbm, sems.at[0]),
        pltpu.make_async_copy(grad_ref, grad_hbm, sems.at[1]),
    ]
    for copy in copies:
        copy.start()
    for copy in copies:
        copy.wait()


def outputs_kernel(
    chances_hbm, grad_hbm, last_chances_hbm, last_grad_hbm, same_ref, other_ref, far_ref, near_ref, own_ref,
    out_hbm, dq_hbm,
    out_ref, dq_ref, chances_ref, grad_ref, sems, in_sems,
):
    kv_heads = out_ref.shape[0]
    height = far_ref.shape[0]
    prompt = 2 * same_ref.shape[0]
    rows = height // PARTS
    heads = out_ref.shape[2] // HEAD_DIM
    refs = (same_ref, other_ref, far_ref, near_ref, own_ref)

    def everywhere(x, part):
        before, after = part * rows, height - (part + 1) * rows
        pieces = [x[:prompt], jnp.zeros((before, x.shape[1]), x.dtype), x[prompt:], jnp.zeros((after, x.shape[1]), x.dtype)]
        return jnp.concatenate([piece for piece in pieces if piece.shape[0]], axis=0)

    def copies(g):
        cols = columns_of(g, heads * HEAD_DIM)
        return (
            pltpu.make_async_copy(out_ref.at[g], out_hbm.at[:, cols], sems.at[0, g]),
            pltpu.make_async_copy(dq_ref.at[g], dq_hbm.at[:, cols], sems.at[1, g]),
        )

    def arrivals(g, chances_from, grad_from):
        return (
            pltpu.make_async_copy(chances_from, chances_ref.at[g], in_sems.at[0, g]),
            pltpu.make_async_copy(grad_from, grad_ref.at[g], in_sems.at[1, g]),
        )

    def stored(g):
        return arrivals(g, chances_hbm.at[g], grad_hbm.at[g])

    last = arrivals(kv_heads - 1, last_chances_hbm, last_grad_hbm)
    for g in range(kv_heads - 1):
        for copy in stored(g):
            copy.start()
    for copy in last:
        copy.start()

    def head(g, arriving):
        for copy in arriving:
            copy.wait()
        keys_t = transposed(stack(refs, columns_of(g)))
        values_t = transposed(stack(refs, columns_of(g + kv_heads)))

        def multiply(part, _):
            out = dot_nn(values_t, everywhere(chances_ref[g, part], part))
            return out, dot_nn(keys_t, everywhere(grad_ref[g, part], part)) * FACTOR

        def turn(part, held):
            for ref, value in zip((out_ref, dq_ref), held):
                value = value.T.astype(BF16)
                for h in range(heads):
                    at = slice(part * rows, (part + 1) * rows)
                    ref[g, at, h * HEAD_DIM : (h + 1) * HEAD_DIM] = value[h * rows : (h + 1) * rows]

        staged(multiply, turn)
        for copy in copies(g):
            copy.start()

    for_heads(kv_heads - 1, lambda g: head(g, stored(g)))
    head(kv_heads - 1, last)
    for g in range(kv_heads):
        for copy in copies(g):
            copy.wait()


def sums_kernel(
    own_ref, near_ref, far_ref, arrived_ref, ak_hbm, av_hbm, pk_hbm, pv_hbm, ak_ref, av_ref, pk_ref, pv_ref, sems
):
    height, columns = ak_ref.shape
    total = arrived_ref[0].astype(F32)
    for chip in range(1, arrived_ref.shape[0]):
        total += arrived_ref[chip].astype(F32)
    pk_ref[...] = total[:, :columns]
    pv_ref[...] = total[:, columns:]
    copies = [pltpu.make_async_copy(pk_ref, pk_hbm, sems.at[0]), pltpu.make_async_copy(pv_ref, pv_hbm, sems.at[1])]
    for copy in copies:
        copy.start()
    even = 1.0 - lax.rem(lax.axis_index("row"), 2).astype(F32)
    near = near_ref[...].astype(F32) * even
    answers = (own_ref[...] + near + far_ref[...].astype(F32)).astype(BF16)
    ak_ref[...] = answers[:, :columns]
    av_ref[...] = answers[:, columns:]
    copies += [pltpu.make_async_copy(ak_ref, ak_hbm, sems.at[2]), pltpu.make_async_copy(av_ref, av_hbm, sems.at[3])]
    for copy in copies[2:]:
        copy.start()
    for copy in copies:
        copy.wait()


def per_device(
    queries, answer_keys, answer_values, prompt_keys, prompt_values, out_grad, weights, lengths
):
    height = queries.shape[0]
    columns = answer_keys.shape[1]
    kv_heads = columns // HEAD_DIM
    span = queries.shape[1] // kv_heads
    size = lax.axis_size("row")
    own_prompt = prompt_keys.shape[0]
    half = own_prompt * size // 2
    prompt = 2 * half
    window = 2 * height + height // PARTS
    lanes = span // HEAD_DIM * height // PARTS
    parts = (kv_heads, PARTS)

    def call(kernel, outs, gflop, arrays, in_specs=None, out_specs=None, scratch=()):
        given = {} if in_specs is None else {"in_specs": in_specs}
        if out_specs is not None:
            given["out_specs"] = out_specs
        return pl.pallas_call(
            kernel,
            out_shape=outs,
            scratch_shapes=list(scratch),
            compiler_params=pltpu.CompilerParams(vmem_limit_bytes=VMEM_LIMIT),
            cost_estimate=pl.CostEstimate(flops=int(gflop * 1e9), bytes_accessed=1_000_000, transcendentals=500_000),
            **given,
        )(*arrays)

    anywhere = pl.BlockSpec(memory_space=pl.ANY)
    vmem = pl.BlockSpec(memory_space=pltpu.VMEM)

    own, spread = pl.pallas_call(
        pack_kernel,
        out_shape=[
            pltpu.VMEM((height, 2 * columns), BF16),
            jax.ShapeDtypeStruct((size // 2, own_prompt, 2 * columns), BF16),
        ],
    )(answer_keys, answer_values, prompt_keys, prompt_values)
    far = shifted(own, 2)
    odd = lax.rem(lax.axis_index("row"), 2) == 1
    near = from_other_core(jnp.where(odd, far, own))
    same = across_chips(spread).reshape(half, 2 * columns)
    near, same = lax.optimization_barrier((near, same))
    other = from_other_core(same)

    def in_hbm(*arrays):
        return [pltpu.with_memory_space_constraint(array, pltpu.HBM) for array in arrays]

    flat_queries, begin, weight_columns = call(
        layout_kernel,
        [
            pltpu.VMEM((*parts, lanes, HEAD_DIM), BF16),
            pltpu.VMEM((PARTS, 8, lanes), F32),
            pltpu.VMEM((height, HEAD_DIM), F32),
        ],
        LAYOUT_GFLOP,
        in_hbm(lengths.reshape(1, -1), weights.reshape(1, -1), queries),
        in_specs=[anywhere] * 3,
        scratch=[
            pltpu.VMEM((1, lengths.shape[0]), jnp.int32),
            pltpu.VMEM((1, height), F32),
            pltpu.VMEM((kv_heads, height, span), BF16),
            pltpu.SemaphoreType.DMA((2,)),
            pltpu.SemaphoreType.DMA((kv_heads,)),
        ],
    )
    cotangent, powers, slopes, stats = call(
        window_kernel,
        [
            pltpu.VMEM((*parts, lanes, HEAD_DIM), BF16),
            pltpu.VMEM((*parts, window, lanes), F32),
            pltpu.VMEM((*parts, window, lanes), F32),
            pltpu.VMEM((*parts, 8, lanes), F32),
        ],
        3,
        [flat_queries, *in_hbm(out_grad), begin, weight_columns, far, near, own],
        in_specs=[vmem, anywhere] + [vmem] * 5,
        scratch=[
            pltpu.VMEM((PARTS, window, lanes), F32),
            pltpu.VMEM((kv_heads, height, span), BF16),
            pltpu.SemaphoreType.DMA((kv_heads,)),
        ],
    )
    keep, passed, near_terms, far_terms, own_terms, chances, score_grad, last_chances, last_grad = call(
        terms_kernel,
        [
            pltpu.VMEM((half, 2 * columns), F32),
            pltpu.VMEM((half, 2 * columns), BF16),
            pltpu.VMEM((height, 2 * columns), BF16),
            pltpu.VMEM((height, 2 * columns), BF16),
            pltpu.VMEM((height, 2 * columns), F32),
            pltpu.HBM((kv_heads - 1, PARTS, prompt + window, lanes), BF16),
            pltpu.HBM((kv_heads - 1, PARTS, prompt + window, lanes), BF16),
            pltpu.VMEM((PARTS, prompt + window, lanes), BF16),
            pltpu.VMEM((PARTS, prompt + window, lanes), BF16),
        ],
        4,
        [flat_queries, cotangent, powers, slopes, stats, same, other],
        out_specs=[vmem] * 5 + [anywhere] * 2 + [vmem] * 2,
        scratch=[pltpu.VMEM((kv_heads - 1, PARTS, prompt + window, lanes), BF16)] * 2
        + [pltpu.VMEM((prompt + 3 * height, HEAD_DIM), F32)] * 2
        + [pltpu.SemaphoreType.DMA((2, kv_heads))],
    )
    last_chances, last_grad = call(
        store_kernel,
        [pltpu.HBM((PARTS, prompt + window, lanes), BF16)] * 2,
        STORE_GFLOP,
        [last_chances, last_grad],
        in_specs=[vmem] * 2,
        out_specs=[anywhere] * 2,
        scratch=[pltpu.SemaphoreType.DMA((2,))],
    )
    near_terms, last_chances = lax.optimization_barrier((from_other_core(near_terms), last_chances))
    whole = jax.ShapeDtypeStruct(queries.shape, BF16)
    attn_out, q_grad = call(
        outputs_kernel,
        [whole, whole],
        OUTPUTS_GFLOP,
        [*in_hbm(chances, score_grad, last_chances, last_grad), same, other, far, near, own],
        in_specs=[anywhere] * 4 + [vmem] * 5,
        out_specs=[anywhere, anywhere],
        scratch=[pltpu.VMEM((kv_heads, height, span), BF16)] * 2
        + [pltpu.VMEM((*parts, prompt + window, lanes), BF16)] * 2
        + [pltpu.SemaphoreType.DMA((2, kv_heads))] * 2,
    )
    far_terms = (far_terms.astype(F32) + jnp.where(odd, near_terms.astype(F32), 0.0)).astype(BF16)
    passed, far_terms = lax.optimization_barrier((passed, far_terms))
    both = (keep + from_other_core(passed).astype(F32)).astype(BF16)
    from_far = shifted(far_terms, -2)
    arrived = across_chips(both.reshape(size // 2, own_prompt, 2 * columns))
    answer_grad = jax.ShapeDtypeStruct((height, columns), BF16)
    prompt_grad = jax.ShapeDtypeStruct((own_prompt, columns), F32)
    dk, dv, dpk, dpv = call(
        sums_kernel,
        [answer_grad, answer_grad, prompt_grad, prompt_grad],
        0.1,
        [own_terms, near_terms, from_far, arrived],
        out_specs=[anywhere] * 4,
        scratch=[pltpu.VMEM((height, columns), BF16)] * 2
        + [pltpu.VMEM((own_prompt, columns), F32)] * 2
        + [pltpu.SemaphoreType.DMA((4,))],
    )
    return attn_out, q_grad, dk, dv, dpk, dpv


def solution(mesh):
    rows = P(("grp", "row"), None)
    return jax.shard_map(
        per_device,
        mesh=mesh,
        in_specs=(rows,) * 6 + (P(("grp", "row")), P("grp")),
        out_specs=(rows,) * 6,
        check_vma=False,
    )
```
